32 devices in a mesh: row: 4 (over y, x), col: 8 (over z, core).
Axes of the slice: x: 2, y: 2, z: 4, core: 2. Of those that a mesh axis runs over, the one named last changes fastest.
Arguments:
- kernel: bfloat16 [4, 4, 8, 2, 256, 256], P('row', None, 'col'), as said below
Outputs:
- panels: float32 [4, 4, 2, 256, 256], P('row')
- schur: bfloat16 [4, 4, 8, 2, 256, 256], P('row', None, 'col')
Inputs may be any that keep to these rules, and one draw needn't show every extreme that they name: kernel describes a symmetric matrix whose leading 2 * 256 rows and columns form a positive definite block.
All inputs are finite; a program needn't handle non-finite values.
Results may differ from the reference program's by a relative error of at most 0.005.
Values may be sent and summed in bfloat16 or wider, within the bound.
No kernel may reach another device: no remote copies, remote signals or barrier semaphores. Data moves between devices by JAX's collectives and lax.ppermute only.
A program may use at most 64 MiB of HBM per device.

```python
import jax
import jax.numpy as jnp
from jax import lax

NB = 256
BC_DEV = 2
PANELS = 2
BR_DEV = 4
ORDER = 4096
N_ROW = 4
N_COL = 8


def draw_kernel(key, part):
    key = jax.random.fold_in(key, 11)
    first_key = jax.random.fold_in(key, 0)
    base = jax.random.uniform(first_key, (ORDER, ORDER), jnp.float32, -1.0, 1.0)
    symmetric = 0.5 * (base + base.T)
    index = jnp.arange(ORDER, dtype=jnp.int32)
    leading = PANELS * NB
    nugget = 2.0 * leading ** 0.5
    on_diagonal = (index[:, None] == index[None, :]) & (index[:, None] < leading)
    symmetric = symmetric + jnp.where(on_diagonal, jnp.float32(nugget), jnp.float32(0.0))
    grid_rows = BR_DEV * N_ROW
    grid_cols = BC_DEV * N_COL
    layout = symmetric.reshape(grid_rows, NB, grid_cols, NB).transpose(0, 2, 1, 3)
    layout = layout.reshape(BR_DEV, N_ROW, BC_DEV, N_COL, NB, NB).transpose(1, 0, 3, 2, 4, 5)
    return layout.astype(jnp.bfloat16)


def setup_inputs(seed: int = 0) -> dict:
    key_of = jax.random.split(jax.random.key(seed), 2)
    return {
        "kernel": draw_kernel(jax.random.fold_in(key_of[1], 71), 0),
    }


def factorize(block):
    lower_factor = jnp.linalg.cholesky(block)
    identity = jnp.eye(block.shape[0], dtype=jnp.float32)
    inverse = lax.linalg.triangular_solve(lower_factor, identity, left_side=True, lower=True)
    return (lower_factor, inverse)

def reference(kernel):
    grid_rows = BR_DEV * N_ROW
    grid_cols = BC_DEV * N_COL
    blocks_all = kernel.transpose(1, 0, 3, 2, 4, 5).reshape(grid_rows, grid_cols, NB, NB)
    matrix = blocks_all.transpose(0, 2, 1, 3).reshape(ORDER, ORDER)
    block_index = jnp.arange(ORDER, dtype=jnp.int32) // NB
    panel_list = []
    for current in range(PANELS):
        start = current * NB
        diagonal = matrix[start:start + NB, start:start + NB].astype(jnp.float32)
        lower_factor, inverse = factorize(diagonal)
        column = matrix[:, start:start + NB].astype(jnp.float32)
        solved = jnp.dot(column, inverse.T, precision=lax.Precision.HIGHEST)
        below = (block_index > current)[:, None]
        strict = jnp.where(below, solved, jnp.zeros((), jnp.float32))
        panel_list.append(strict.at[start:start + NB].set(lower_factor))
        rounded = strict.astype(jnp.bfloat16)

        def update_rows(pair, rounded=rounded):
            rows_now, left_rows = pair
            change = jnp.dot(left_rows.astype(jnp.float32), rounded.T.astype(jnp.float32), preferred_element_type=jnp.float32)
            return (rows_now.astype(jnp.float32) - change).astype(jnp.bfloat16)
        matrix = lax.map(update_rows, (matrix.reshape(grid_rows, NB, ORDER), rounded.reshape(grid_rows, NB, NB)))
        matrix = matrix.reshape(ORDER, ORDER)
    keep = (block_index[:, None] >= PANELS) & (block_index[None, :] >= PANELS)
    schur = jnp.where(keep, matrix, jnp.zeros((), jnp.bfloat16))
    schur = schur.reshape(grid_rows, NB, grid_cols, NB).transpose(0, 2, 1, 3)
    schur = schur.reshape(BR_DEV, N_ROW, BC_DEV, N_COL, NB, NB).transpose(1, 0, 3, 2, 4, 5)
    panels = jnp.stack([piece.reshape(grid_rows, NB, NB) for piece in panel_list], axis=1)
    panels = panels.reshape(BR_DEV, N_ROW, PANELS, NB, NB).transpose(1, 0, 2, 3, 4)
    return (panels, schur)
```

```python
import jax
import jax.numpy as jnp
from jax import lax
from jax.experimental import pallas as pl
from jax.experimental.pallas import tpu as pltpu
from jax.sharding import PartitionSpec as P

PANELS = 2
HIGHEST = lax.Precision.HIGHEST
VMEM_LIMIT = 48 * 1024 * 1024


def reciprocal(x):
    r = pl.reciprocal(x, approx=True)
    return r * (2.0 - x * r)

def spread(row):
    return jnp.broadcast_to(row, (8, row.shape[1]))

def lane(tile, k):
    return jnp.broadcast_to(tile[:, k:k + 1], (8, 128))

def factor_tile(matrix):
    groups = 16
    rows_of = lax.broadcasted_iota(jnp.int32, (8, 128), 0)
    cols_of = lax.broadcasted_iota(jnp.int32, (8, 128), 1)
    left = [matrix[8 * g:8 * g + 8, :] for g in range(groups)]
    right = [(cols_of == rows_of + 8 * g).astype(jnp.float32) for g in range(groups)]
    upper, inverse = [], []
    for s in range(groups):
        y = [spread(left[s][k:k + 1, :]) for k in range(8)]
        v = [spread(right[s][k:k + 1, :]) for k in range(8)]
        d = [[lane(y[i], 8 * s + k) if k >= i else None for k in range(8)] for i in range(8)]
        ratio = [[None] * 8 for _ in range(8)]
        inv = []
        for k in range(8):
            inv.append(reciprocal(d[k][k]))
            for i in range(k + 1, 8):
                ratio[i][k] = d[k][i] * inv[k]
                for j in range(i, 8):
                    d[i][j] = d[i][j] - ratio[i][k] * d[k][j]
                y[i] = y[i] - ratio[i][k] * y[k]
                v[i] = v[i] - ratio[i][k] * v[k]
        up = jnp.zeros((8, 128), jnp.float32)
        low = jnp.zeros((8, 128), jnp.float32)
        for k in range(8):
            root = lax.rsqrt(d[k][k])
            up = jnp.where(rows_of == k, y[k] * root, up)
            low = jnp.where(rows_of == k, v[k] * root, low)
        upper.append(jnp.where(cols_of >= rows_of + 8 * s, up, 0.0))
        inverse.append(low)
        if s + 1 == groups:
            break
        x, w = [None] * 8, [None] * 8
        for k in reversed(range(8)):
            x[k] = y[k] * inv[k]
            w[k] = v[k] * inv[k]
            for j in range(k + 1, 8):
                x[k] = x[k] - ratio[j][k] * x[j]
                w[k] = w[k] - ratio[j][k] * w[j]
        for g in range(s + 1, groups):
            f = [lane(left[g], 8 * s + k) for k in range(8)]
            for k in range(8):
                left[g] = left[g] - f[k] * x[k]
                right[g] = right[g] - f[k] * w[k]
    return jnp.concatenate(upper, axis=0), jnp.concatenate(inverse, axis=0)

def dot(a, b, dims=((1,), (0,))):
    return lax.dot_general(a, b, (dims, ((), ())), precision=HIGHEST, preferred_element_type=jnp.float32)

ROWS = ((1,), (1,))

def factor_rest(upper_1, inv_1, side, rest, lower_ref, inverse_ref):
    half = side.shape[0]
    lower_21 = dot(side, inv_1, ROWS)
    rest = rest - dot(lower_21, lower_21, ROWS)
    beside = dot(lower_21, inv_1)
    upper_2, inv_2 = factor_tile(rest)
    zero = jnp.zeros((half, half), jnp.float32)
    lower_ref[:half, :half] = upper_1.T
    lower_ref[:half, half:] = zero
    lower_ref[half:, :half] = lower_21
    lower_ref[half:, half:] = upper_2.T
    inverse_ref[:half, :half] = inv_1
    inverse_ref[:half, half:] = zero
    inverse_ref[half:, :half] = -dot(inv_2, beside)
    inverse_ref[half:, half:] = inv_2


def mul(a, b, dims=((1,), (0,))):
    return lax.dot_general(a, b, (dims, ((), ())), preferred_element_type=jnp.float32)


def start_kernel(quarter_ref, upper_ref, inverse_ref):
    upper, inverse = factor_tile(quarter_ref[...].astype(jnp.float32))
    upper_ref[...] = upper
    inverse_ref[...] = inverse


def first_kernel(rest_ref, upper_ref, tile_inverse_ref, lower_ref, inverse_ref):
    half = rest_ref.shape[1]
    side = rest_ref[:half].astype(jnp.float32)
    rest = rest_ref[half:].astype(jnp.float32)
    factor_rest(upper_ref[...], tile_inverse_ref[...], side, rest, lower_ref, inverse_ref)


def second_kernel(
    top_10_ref, rest_10_ref, rest_01_ref, top_11_ref, rest_11_ref, inverse_0_ref, panel_ref, lower_ref, inverse_ref,
):
    half = top_11_ref.shape[1]
    left = jnp.concatenate([top_10_ref[...], rest_10_ref[:half]], axis=0).astype(jnp.float32)
    right = jnp.concatenate([rest_01_ref[:half].astype(jnp.float32).T, rest_10_ref[half:].astype(jnp.float32)], axis=0)
    panel = dot(jnp.concatenate([left, right], axis=1), inverse_0_ref[...], ROWS).astype(jnp.bfloat16)
    panel_ref[...] = panel
    above, below = panel[:half], panel[half:]
    top = (top_11_ref[...].astype(jnp.float32) - mul(above, above, ROWS)).astype(jnp.bfloat16)
    side = (rest_11_ref[:half].astype(jnp.float32) - mul(below, above, ROWS)).astype(jnp.bfloat16)
    rest = (rest_11_ref[half:].astype(jnp.float32) - mul(below, below, ROWS)).astype(jnp.bfloat16)
    upper, inverse = factor_tile(top.astype(jnp.float32))
    factor_rest(upper, inverse, side.astype(jnp.float32), rest.astype(jnp.float32), lower_ref, inverse_ref)


def split(x, pieces_ref):
    for piece in range(3):
        high = x.astype(jnp.bfloat16)
        pieces_ref[piece] = high
        x = x - high.astype(jnp.float32)


def update_kernel(
    ids_ref, column_0_ref, column_1_ref, above_0_ref, above_1_ref, blocks_ref,
    lower_0_ref, lower_1_ref, inverse_0_ref, inverse_1_ref, panel_10_ref,
    panels_ref, schur_ref, pieces_0_ref, pieces_1_ref, mirror_0_ref, mirror_1_ref,
):
    step = pl.program_id(0)
    col_blocks = blocks_ref.shape[1]

    @pl.when(step == 0)
    def _():
        split(inverse_0_ref[...], pieces_0_ref)
        split(inverse_1_ref[...], pieces_1_ref)
        for m in range(col_blocks):
            above = above_0_ref[m]
            mirror = sum(mul(pieces_0_ref[p], above) for p in (2, 1, 0)).astype(jnp.bfloat16)
            mirror_0_ref[m] = mirror
            above = above_1_ref[m].astype(jnp.float32) - mul(panel_10_ref[...], mirror)
            above = above.astype(jnp.bfloat16)
            mirror_1_ref[m] = sum(mul(pieces_1_ref[p], above) for p in (2, 1, 0)).astype(jnp.bfloat16)

    block_row = step * ids_ref[2] + ids_ref[0]
    column = column_0_ref[0]
    solved = sum(mul(column, pieces_0_ref[p], ROWS) for p in (2, 1, 0))
    solved = jnp.where(block_row > 0, solved, 0.0)
    rounded_0 = solved.astype(jnp.bfloat16)
    panels_ref[0, 0] = jnp.where(block_row == 0, lower_0_ref[...], solved)
    column = column_1_ref[0].astype(jnp.float32) - mul(rounded_0, panel_10_ref[...], ROWS)
    column = column.astype(jnp.bfloat16)
    solved = sum(mul(column, pieces_1_ref[p], ROWS) for p in (2, 1, 0))
    solved = jnp.where(block_row > 1, solved, 0.0)
    rounded_1 = solved.astype(jnp.bfloat16)
    panels_ref[0, 1] = jnp.where(block_row == 1, lower_1_ref[...], solved)
    for m in range(col_blocks):
        block = blocks_ref[0, m].astype(jnp.float32) - mul(rounded_0, mirror_0_ref[m])
        block = block.astype(jnp.bfloat16).astype(jnp.float32) - mul(rounded_1, mirror_1_ref[m])
        keep = (block_row >= PANELS) & (m * ids_ref[3] + ids_ref[1] >= PANELS)
        schur_ref[0, m] = jnp.where(keep, block, 0.0).astype(jnp.bfloat16)


FACTOR_COST = pl.CostEstimate(flops=10**6, bytes_accessed=10**4, transcendentals=0)


def call_factor(kernel, name, shapes, *operands):
    return pl.pallas_call(
        kernel, out_shape=shapes, name=name, cost_estimate=FACTOR_COST,
        compiler_params=pltpu.CompilerParams(vmem_limit_bytes=VMEM_LIMIT),
    )(*operands)


def square(width, dtype=jnp.float32):
    return jax.ShapeDtypeStruct((width, width), dtype)


def update(ids, column_0, column_1, above_0, above_1, blocks, lower_0, lower_1, inverse_0, inverse_1, panel_10):
    row_blocks, col_blocks, width = blocks.shape[:3]
    one_row = pl.BlockSpec((1, width, width), lambda i: (i, 0, 0))
    whole_square = pl.BlockSpec((width, width), lambda i: (0, 0))
    above_spec = pl.BlockSpec((col_blocks, width, width), lambda i: (0, 0, 0))
    block_spec = pl.BlockSpec((1, col_blocks, width, width), lambda i: (i, 0, 0, 0))
    return pl.pallas_call(
        update_kernel,
        grid=(row_blocks,),
        in_specs=[pl.BlockSpec(memory_space=pltpu.SMEM), one_row, one_row, above_spec, above_spec, block_spec]
        + [whole_square] * 5,
        out_specs=[pl.BlockSpec((1, PANELS, width, width), lambda i: (i, 0, 0, 0)), block_spec],
        out_shape=[
            jax.ShapeDtypeStruct((row_blocks, PANELS, width, width), jnp.float32),
            jax.ShapeDtypeStruct(blocks.shape, jnp.bfloat16),
        ],
        scratch_shapes=[
            pltpu.VMEM((3, width, width), jnp.bfloat16),
            pltpu.VMEM((3, width, width), jnp.bfloat16),
            pltpu.VMEM((col_blocks, width, width), jnp.bfloat16),
            pltpu.VMEM((col_blocks, width, width), jnp.bfloat16),
        ],
        compiler_params=pltpu.CompilerParams(vmem_limit_bytes=VMEM_LIMIT),
        cost_estimate=pl.CostEstimate(flops=2 * 10**9, bytes_accessed=6 * 10**6, transcendentals=0),
        name="solve_and_update",
    )(ids, column_0, column_1, above_0, above_1, blocks, lower_0, lower_1, inverse_0, inverse_1, panel_10)


def corner_kernel(kernel_ref, quarters_ref, semaphores):
    half = quarters_ref.shape[1]
    copies = []
    for q, (row, col) in enumerate(((0, 0), (1, 0), (1, 1))):
        source = kernel_ref.at[0, 0, 0, 0, pl.ds(row * half, half), pl.ds(col * half, half)]
        copies.append(pltpu.make_async_copy(source, quarters_ref.at[pl.ds(q * half, half)], semaphores.at[q]))
    for copy in copies:
        copy.start()
    for copy in copies:
        copy.wait()


def corner_quarters(kernel):
    half = kernel.shape[-1] // 2
    return pl.pallas_call(
        corner_kernel,
        in_specs=[pl.BlockSpec(memory_space=pltpu.HBM)],
        out_specs=pl.BlockSpec(memory_space=pltpu.VMEM),
        out_shape=jax.ShapeDtypeStruct((3 * half, half), kernel.dtype),
        scratch_shapes=[pltpu.SemaphoreType.DMA((3,))],
        compiler_params=pltpu.CompilerParams(vmem_limit_bytes=60 * 1024 * 1024),
        name="corner_quarters",
    )(kernel)


def swap(block, axis, distance):
    count = lax.axis_size(axis)
    return lax.ppermute(block, axis, [(d, d ^ distance) for d in range(count)])


HOLDERS = ((0, 0), (0, 1), (1, 0), (1, 1))


def diagonal_along(quarters, my_col):
    col_count = lax.axis_size("col")
    along = quarters
    for chip in range(1, col_count // 2):
        pairs = [(r * col_count + core, r * col_count + chip * 2 + core) for r, core in HOLDERS]
        got = lax.ppermute(quarters, ("row", "col"), pairs)
        along = jnp.where(my_col // 2 == chip, got, along)
    return along


def diagonal_down(along, my_row, my_col):
    row_count, col_count = lax.axis_size("row"), lax.axis_size("col")
    first, second = along, along
    for step in range(1, row_count):
        pairs = []
        for chip in range(col_count // 2):
            for r, core in HOLDERS:
                col = chip * 2 + core
                pairs.append((r * col_count + col, (step ^ r) * col_count + col))
        got = lax.ppermute(along, ("row", "col"), pairs)
        first = jnp.where(my_row == step, got, first)
        second = jnp.where(my_row == step ^ 1, got, second)
    pair = jnp.stack([first, second])
    other = swap(pair, "col", 1)
    even = my_col % 2 == 0
    left = jnp.where(even, pair, other)
    right = jnp.where(even, other, pair)
    return left[0], right[0], left[1], right[1]


def rows_down(block, my_row):
    reach = 2
    while reach < lax.axis_size("row"):
        got = swap(block, "row", reach)
        block = jnp.where((my_row >= reach) & (my_row < 2 * reach), got, block)
        reach *= 2
    return block


def row_swap(block, my_row):
    other = swap(block, "row", 1)
    even = my_row % 2 == 0
    return jnp.where(even, block, other), jnp.where(even, other, block)


def first_stride(block):
    chips = lax.axis_size("col") // 2
    pairs = [(core, core + chips) for core in range(2)]
    return block, lax.ppermute(block, "col", pairs)


def other_strides(block, got, my_col):
    chips = lax.axis_size("col") // 2
    stride = chips // 2
    while True:
        block = jnp.where((my_col // 2) % (2 * stride) == stride, got, block)
        stride //= 2
        if stride == 0:
            return block
        if stride == 1:
            got = swap(block, "col", 2)
        else:
            sources = [chip * 2 + core for chip in range(0, chips, 2 * stride) for core in range(2)]
            got = lax.ppermute(block, "col", [(s, s + 2 * stride) for s in sources])


def per_device(kernel):
    my_row = lax.axis_index("row")
    my_col = lax.axis_index("col")
    even = my_col % 2 == 0
    blocks = kernel[0, :, 0]
    width = blocks.shape[2]
    half = width // 2
    quarters = corner_quarters(kernel)
    along = diagonal_along(quarters, my_col)
    rows, along = lax.optimization_barrier((blocks[:, 0], along))
    rows, rows_got = first_stride(rows)
    block_00, block_01, block_10, block_11 = diagonal_down(along, my_row, my_col)
    above, block_00 = lax.optimization_barrier((blocks[0], block_00))
    above = rows_down(above, my_row)
    upper_0, tile_inverse_0 = call_factor(start_kernel, "factor_start", [square(half)] * 2, block_00[:half])
    rows, rows_got, tile_inverse_0 = lax.optimization_barrier((rows, rows_got, tile_inverse_0))
    rows = other_strides(rows, rows_got, my_col)
    lower_0, inverse_0 = call_factor(
        first_kernel, "factor_first", [square(width)] * 2, block_00[half:], upper_0, tile_inverse_0)
    above, inverse_0 = lax.optimization_barrier((above, inverse_0))
    above_0, above_1 = row_swap(above, my_row)
    panel_10, lower_1, inverse_1 = call_factor(
        second_kernel, "factor_second", [square(width, jnp.bfloat16)] + [square(width)] * 2,
        block_10[:half], block_10[half:], block_01[half:], block_11[:half], block_11[half:], inverse_0)
    rows, above_0, above_1, inverse_1 = lax.optimization_barrier((rows, above_0, above_1, inverse_1))
    other = swap(rows, "col", 1)
    column_0 = jnp.where(even, rows, other)
    column_1 = jnp.where(even, other, rows)
    ids = jnp.stack([my_row, my_col, lax.axis_size("row"), lax.axis_size("col")]).astype(jnp.int32)
    panels, schur = update(
        ids, column_0, column_1, above_0, above_1, blocks,
        lower_0, lower_1, inverse_0, inverse_1, panel_10,
    )
    return (panels[None], schur[None, :, None])


def solution(mesh):
    in_specs = (P("row", None, "col", None, None, None),)
    out_specs = (P("row", None, None, None, None), P("row", None, "col", None, None, None))
    return jax.shard_map(
        per_device, mesh=mesh, in_specs=in_specs, out_specs=out_specs, check_vma=False
    )
```

```python
import jax
import jax.numpy as jnp
from jax import lax
from jax.experimental import pallas as pl
from jax.experimental.pallas import tpu as pltpu
from jax.sharding import PartitionSpec as P

PANELS = 2
HIGHEST = lax.Precision.HIGHEST
VMEM_LIMIT = 48 * 1024 * 1024

def spread(row):
    return jnp.broadcast_to(row, (8, row.shape[1]))


def lane(tile, k):
    return jnp.broadcast_to(tile[:, k:k + 1], (8, 128))


def factor_tile(matrix):
    groups = 16
    rows_of = lax.broadcasted_iota(jnp.int32, (8, 128), 0)
    cols_of = lax.broadcasted_iota(jnp.int32, (8, 128), 1)
    left = [matrix[8 * g:8 * g + 8, :] for g in range(groups)]
    right = [(cols_of == rows_of + 8 * g).astype(jnp.float32) for g in range(groups)]
    upper, inverse = [], []
    for s in range(groups):
        y = [spread(left[s][k:k + 1, :]) for k in range(8)]
        v = [spread(right[s][k:k + 1, :]) for k in range(8)]
        d = [[lane(y[i], 8 * s + k) if k >= i else None for k in range(8)] for i in range(8)]
        last = s + 1 == groups
        columns = [[lane(left[g], 8 * s + k) for k in range(8)] for g in range(s + 1, groups)]
        e = list(columns[0]) if not last else None
        ratio = [[None] * 8 for _ in range(8)]
        inv = []
        for k in range(8):
            guess = pl.reciprocal(d[k][k], approx=True)
            correction = 2.0 - d[k][k] * guess
            inv.append(guess * correction)
            if k < 7:
                for j in range(k + 1, 8):
                    d[k + 1][j] = d[k + 1][j] - d[k][k + 1] * guess * d[k][j] * correction
            for i in range(k + 1, 8):
                ratio[i][k] = d[k][i] * inv[k]
                if i > k + 1:
                    for j in range(i, 8):
                        d[i][j] = d[i][j] - ratio[i][k] * d[k][j]
                y[i] = y[i] - ratio[i][k] * y[k]
                v[i] = v[i] - ratio[i][k] * v[k]
            if not last:
                left[s + 1] = left[s + 1] - e[k] * guess * y[k] * correction
                for j in range(k + 1, 8):
                    e[j] = e[j] - e[k] * ratio[j][k]
        up = jnp.zeros((8, 128), jnp.float32)
        low = jnp.zeros((8, 128), jnp.float32)
        for k in range(8):
            root = lax.rsqrt(d[k][k])
            up = jnp.where(rows_of == k, y[k] * root, up)
            low = jnp.where(rows_of == k, v[k] * root, low)
        upper.append(jnp.where(cols_of >= rows_of + 8 * s, up, 0.0))
        inverse.append(low)
        if last:
            break
        x, w = [None] * 8, [None] * 8
        for k in reversed(range(8)):
            x[k] = y[k] * inv[k]
            w[k] = v[k] * inv[k]
            for j in reversed(range(k + 1, 8)):
                x[k] = x[k] - ratio[j][k] * x[j]
                w[k] = w[k] - ratio[j][k] * w[j]
        for g in range(s + 1, groups):
            f = columns[g - s - 1]
            for k in reversed(range(8)):
                if g > s + 1:
                    left[g] = left[g] - f[k] * x[k]
                right[g] = right[g] - f[k] * w[k]
    return jnp.concatenate(upper, axis=0), jnp.concatenate(inverse, axis=0)


def dot(a, b, dims=((1,), (0,))):
    return lax.dot_general(a, b, (dims, ((), ())), precision=HIGHEST, preferred_element_type=jnp.float32)

ROWS = ((1,), (1,))

def factor_rest(upper_1, inv_1, side, rest, lower_ref, inverse_ref):
    half = side.shape[0]
    lower_21 = dot(side, inv_1, ROWS)
    rest = rest - dot(lower_21, lower_21, ROWS)
    beside = dot(lower_21, inv_1)
    upper_2, inv_2 = factor_tile(rest)
    zero = jnp.zeros((half, half), jnp.float32)
    lower_ref[:half, :half] = upper_1.T
    lower_ref[:half, half:] = zero
    lower_ref[half:, :half] = lower_21
    lower_ref[half:, half:] = upper_2.T
    inverse_ref[:half, :half] = inv_1
    inverse_ref[:half, half:] = zero
    inverse_ref[half:, :half] = -dot(inv_2, beside)
    inverse_ref[half:, half:] = inv_2


def mul(a, b, dims=((1,), (0,))):
    return lax.dot_general(a, b, (dims, ((), ())), preferred_element_type=jnp.float32)


def start_kernel(quarter_ref, upper_ref, inverse_ref):
    upper, inverse = factor_tile(quarter_ref[...].astype(jnp.float32))
    upper_ref[...] = upper
    inverse_ref[...] = inverse


def first_kernel(rest_ref, upper_ref, tile_inverse_ref, lower_ref, inverse_ref):
    half = rest_ref.shape[1]
    side = rest_ref[:half].astype(jnp.float32)
    rest = rest_ref[half:].astype(jnp.float32)
    factor_rest(upper_ref[...], tile_inverse_ref[...], side, rest, lower_ref, inverse_ref)


def second_start_kernel(
    top_10_ref, rest_10_ref, rest_01_ref, top_11_ref, rest_11_ref, inverse_0_ref,
    panel_ref, later_ref, upper_ref, inverse_ref,
):
    half = top_11_ref.shape[1]
    left = jnp.concatenate([top_10_ref[...], rest_10_ref[:half]], axis=0).astype(jnp.float32)
    right = jnp.concatenate([rest_01_ref[:half].astype(jnp.float32).T, rest_10_ref[half:].astype(jnp.float32)], axis=0)
    panel = dot(jnp.concatenate([left, right], axis=1), inverse_0_ref[...], ROWS).astype(jnp.bfloat16)
    panel_ref[...] = panel
    above, below = panel[:half], panel[half:]
    top = (top_11_ref[...].astype(jnp.float32) - mul(above, above, ROWS)).astype(jnp.bfloat16)
    later_ref[:half] = (rest_11_ref[:half].astype(jnp.float32) - mul(below, above, ROWS)).astype(jnp.bfloat16)
    later_ref[half:] = (rest_11_ref[half:].astype(jnp.float32) - mul(below, below, ROWS)).astype(jnp.bfloat16)
    upper, inverse = factor_tile(top.astype(jnp.float32))
    upper_ref[...] = upper
    inverse_ref[...] = inverse


def second_kernel(
    rest_ref, upper_ref, tile_inverse_ref, inverse_0_ref, panel_ref, above_0_ref, above_1_ref,
    lower_ref, pieces_0_ref, pieces_1_ref, mirror_ref, later_ref, inverse_ref,
):
    split(inverse_0_ref[...], pieces_0_ref)
    for m in range(above_0_ref.shape[0]):
        mirror = product(pieces_0_ref, above_0_ref[m]).astype(jnp.bfloat16)
        mirror_ref[m] = mirror
        later = above_1_ref[m].astype(jnp.float32) - mul(panel_ref[...], mirror)
        later_ref[m] = later.astype(jnp.bfloat16)
    first_kernel(rest_ref, upper_ref, tile_inverse_ref, lower_ref, inverse_ref)
    split(inverse_ref[...], pieces_1_ref)


def product(pieces_ref, block):
    return sum(mul(pieces_ref[p], block) for p in (2, 1, 0))


def solve(rows, pieces_ref):
    return sum(mul(rows, pieces_ref[p], ROWS) for p in (2, 1, 0))


def split(x, pieces_ref):
    for piece in range(3):
        high = x.astype(jnp.bfloat16)
        pieces_ref[piece] = high
        x = x - high.astype(jnp.float32)


def update_kernel(
    ids_ref, column_0_ref, column_1_ref, blocks_ref, mirror_0_ref, later_ref,
    lower_0_ref, lower_1_ref, pieces_0_ref, pieces_1_ref, panel_10_ref,
    panels_ref, schur_ref, mirror_1_ref,
):
    step = pl.program_id(0)
    batch, col_blocks, width = blocks_ref.shape[:3]

    @pl.when(step == 0)
    def _():
        for m in range(col_blocks):
            mirror_1_ref[m] = product(pieces_1_ref, later_ref[m]).astype(jnp.bfloat16)

    ids = [(step * batch + i) * ids_ref[2] + ids_ref[0] for i in range(batch)]

    def below(solved, panel, lower_ref):
        parts = []
        for i, block_row in enumerate(ids):
            part = jnp.where(block_row > panel, solved[i * width:(i + 1) * width], 0.0)
            panels_ref[i, panel] = jnp.where(block_row == panel, lower_ref[...], part)
            parts.append(part)
        return jnp.concatenate(parts, axis=0).astype(jnp.bfloat16)

    rounded_0 = below(solve(column_0_ref[...].reshape(batch * width, width), pieces_0_ref), 0, lower_0_ref)
    column = column_1_ref[...].reshape(batch * width, width).astype(jnp.float32)
    column = (column - mul(rounded_0, panel_10_ref[...], ROWS)).astype(jnp.bfloat16)
    rounded_1 = below(solve(column, pieces_1_ref), 1, lower_1_ref)
    for m in range(col_blocks):
        change_0 = mul(rounded_0, mirror_0_ref[m])
        change_1 = mul(rounded_1, mirror_1_ref[m])
        for i, block_row in enumerate(ids):
            part = slice(i * width, (i + 1) * width)
            block = blocks_ref[i, m].astype(jnp.float32) - change_0[part]
            block = block.astype(jnp.bfloat16).astype(jnp.float32) - change_1[part]
            keep = (block_row >= PANELS) & (m * ids_ref[3] + ids_ref[1] >= PANELS)
            schur_ref[i, m] = jnp.where(keep, block, 0.0).astype(jnp.bfloat16)


FACTOR_COST = pl.CostEstimate(flops=10**6, bytes_accessed=10**4, transcendentals=0)


def call_factor(kernel, name, shapes, *operands):
    return pl.pallas_call(
        kernel, out_shape=shapes, name=name, cost_estimate=FACTOR_COST,
        compiler_params=pltpu.CompilerParams(vmem_limit_bytes=VMEM_LIMIT),
    )(*operands)


def square(width, dtype=jnp.float32):
    return jax.ShapeDtypeStruct((width, width), dtype)


def update(ids, column_0, column_1, blocks, mirror_0, later, lower_0, lower_1, pieces_0, pieces_1, panel_10):
    row_blocks, col_blocks, width = blocks.shape[:3]
    batch = 2 if row_blocks % 2 == 0 else 1
    rows_spec = pl.BlockSpec((batch, width, width), lambda i: (i, 0, 0))
    square_spec = pl.BlockSpec((width, width), lambda i: (0, 0))
    mirror_spec = pl.BlockSpec((col_blocks, width, width), lambda i: (0, 0, 0))
    pieces_spec = pl.BlockSpec((3, width, width), lambda i: (0, 0, 0))
    block_spec = pl.BlockSpec((batch, col_blocks, width, width), lambda i: (i, 0, 0, 0))
    return pl.pallas_call(
        update_kernel,
        grid=(row_blocks // batch,),
        in_specs=[pl.BlockSpec(memory_space=pltpu.SMEM), rows_spec, rows_spec, block_spec, mirror_spec, mirror_spec]
        + [square_spec] * 2 + [pieces_spec] * 2 + [square_spec],
        out_specs=[pl.BlockSpec((batch, PANELS, width, width), lambda i: (i, 0, 0, 0)), block_spec],
        out_shape=[
            jax.ShapeDtypeStruct((row_blocks, PANELS, width, width), jnp.float32),
            jax.ShapeDtypeStruct(blocks.shape, jnp.bfloat16),
        ],
        scratch_shapes=[pltpu.VMEM((col_blocks, width, width), jnp.bfloat16)],
        compiler_params=pltpu.CompilerParams(vmem_limit_bytes=VMEM_LIMIT),
        cost_estimate=pl.CostEstimate(flops=2 * 10**9, bytes_accessed=6 * 10**6, transcendentals=0),
        name="solve_and_update",
    )(ids, column_0, column_1, blocks, mirror_0, later, lower_0, lower_1, pieces_0, pieces_1, panel_10)


def pack_kernel(kernel_ref, quarters_ref, semaphores):
    half = quarters_ref.shape[1]
    copies = []
    for q, (row, col) in enumerate(((0, 0), (1, 0), (1, 1))):
        source = kernel_ref.at[0, 0, 0, 0, pl.ds(row * half, half), pl.ds(col * half, half)]
        copies.append(pltpu.make_async_copy(source, quarters_ref.at[pl.ds(q * half, half)], semaphores.at[q]))
    for copy in copies:
        copy.start()
    for copy in copies:
        copy.wait()


def pack(kernel):
    half = kernel.shape[-1] // 2
    return pl.pallas_call(
        pack_kernel,
        in_specs=[pl.BlockSpec(memory_space=pltpu.HBM)],
        out_shape=jax.ShapeDtypeStruct((3 * half, half), kernel.dtype),
        scratch_shapes=[pltpu.SemaphoreType.DMA((3,))],
        compiler_params=pltpu.CompilerParams(vmem_limit_bytes=2 * 1024 * 1024),
        name="pack",
    )(kernel)


def swap(block, axis, distance):
    count = lax.axis_size(axis)
    return lax.ppermute(block, axis, [(d, d ^ distance) for d in range(count)])


HOLDERS = ((0, 0), (0, 1), (1, 0), (1, 1))


def diagonal_along(quarters, my_col):
    col_count = lax.axis_size("col")
    along = quarters
    for chip in range(1, col_count // 2):
        pairs = [(r * col_count + core, r * col_count + chip * 2 + core) for r, core in HOLDERS]
        got = lax.ppermute(quarters, ("row", "col"), pairs)
        along = jnp.where(my_col // 2 == chip, got, along)
    return along


def diagonal_down(along, my_row):
    row_count, col_count = lax.axis_size("row"), lax.axis_size("col")
    first, second = along, along
    for step in range(1, row_count):
        pairs = []
        for chip in range(col_count // 2):
            for r, core in HOLDERS:
                col = chip * 2 + core
                pairs.append((r * col_count + col, (step ^ r) * col_count + col))
        got = lax.ppermute(along, ("row", "col"), pairs)
        first = jnp.where(my_row == step, got, first)
        second = jnp.where(my_row == step ^ 1, got, second)
    return jnp.stack([first, second])


def both_cores(pair, my_col):
    other = swap(pair, "col", 1)
    even = my_col % 2 == 0
    left = jnp.where(even, pair, other)
    right = jnp.where(even, other, pair)
    return left[0], right[0], left[1], right[1]


def first_reach(block):
    return block, swap(block, "row", 2)


def other_reaches(block, got, my_row):
    reach = 2
    while True:
        block = jnp.where((my_row >= reach) & (my_row < 2 * reach), got, block)
        reach *= 2
        if reach >= lax.axis_size("row"):
            return block
        got = swap(block, "row", reach)


def by_row(block, other, my_row):
    even = my_row % 2 == 0
    return jnp.where(even, block, other), jnp.where(even, other, block)


def first_stride(block):
    chips = lax.axis_size("col") // 2
    pairs = [(core, core + chips) for core in range(2)]
    return block, lax.ppermute(block, "col", pairs)


def other_strides(block, got, my_col):
    chips = lax.axis_size("col") // 2
    stride = chips // 2
    while True:
        block = jnp.where((my_col // 2) % (2 * stride) == stride, got, block)
        stride //= 2
        if stride == 0:
            return block
        if stride == 1:
            got = swap(block, "col", 2)
        else:
            sources = [chip * 2 + core for chip in range(0, chips, 2 * stride) for core in range(2)]
            got = lax.ppermute(block, "col", [(s, s + 2 * stride) for s in sources])


def per_device(kernel):
    my_row = lax.axis_index("row")
    my_col = lax.axis_index("col")
    even = my_col % 2 == 0
    blocks = kernel[0, :, 0]
    col_blocks, width = blocks.shape[1:3]
    half = width // 2
    quarters = pack(kernel)
    rows, above, _ = lax.optimization_barrier((blocks[:, 0], blocks[0], quarters))
    rows, rows_got = first_stride(rows)
    above, above_got = first_reach(above)
    along = diagonal_along(quarters, my_col)
    pair = diagonal_down(along, my_row)
    pair, rows, rows_got = lax.optimization_barrier((pair, rows, rows_got))
    block_00, block_01, block_10, block_11 = both_cores(pair, my_col)
    rows = other_strides(rows, rows_got, my_col)
    upper_0, tile_inverse_0 = call_factor(start_kernel, "factor_start", [square(half)] * 2, block_00[:half])
    above, above_got, tile_inverse_0 = lax.optimization_barrier((above, above_got, tile_inverse_0))
    above = other_reaches(above, above_got, my_row)
    above_other = swap(above, "row", 1)
    lower_0, inverse_0 = call_factor(
        first_kernel, "factor_first", [square(width)] * 2, block_00[half:], upper_0, tile_inverse_0)
    panel_10, rest_11, upper_1, tile_inverse_1 = call_factor(
        second_start_kernel, "factor_second_start",
        [square(width, jnp.bfloat16), jax.ShapeDtypeStruct((width, half), jnp.bfloat16), square(half), square(half)],
        block_10[:half], block_10[half:], block_01[half:], block_11[:half], block_11[half:], inverse_0)
    rows, above, above_other, tile_inverse_1 = lax.optimization_barrier((rows, above, above_other, tile_inverse_1))
    above_0, above_1 = by_row(above, above_other, my_row)
    other = swap(rows, "col", 1)
    pieces = jax.ShapeDtypeStruct((3, width, width), jnp.bfloat16)
    mirror = jax.ShapeDtypeStruct((col_blocks, width, width), jnp.bfloat16)
    lower_1, pieces_0, pieces_1, mirror_0, later, _ = call_factor(
        second_kernel, "factor_second", [square(width), pieces, pieces, mirror, mirror, square(width)],
        rest_11, upper_1, tile_inverse_1, inverse_0, panel_10, above_0, above_1)
    other, lower_1 = lax.optimization_barrier((other, lower_1))
    column_0 = jnp.where(even, rows, other)
    column_1 = jnp.where(even, other, rows)
    ids = jnp.stack([my_row, my_col, lax.axis_size("row"), lax.axis_size("col")]).astype(jnp.int32)
    panels, schur = update(
        ids, column_0, column_1, blocks, mirror_0, later, lower_0, lower_1, pieces_0, pieces_1, panel_10)
    return (panels[None], schur[None, :, None])


def solution(mesh):
    in_specs = (P("row", None, "col", None, None, None),)
    out_specs = (P("row", None, None, None, None), P("row", None, "col", None, None, None))
    return jax.shard_map(
        per_device, mesh=mesh, in_specs=in_specs, out_specs=out_specs, check_vma=False
    )
```

```python
import jax
import jax.numpy as jnp
from jax import lax
from jax.experimental import pallas as pl
from jax.experimental.pallas import tpu as pltpu
from jax.sharding import PartitionSpec as P

PANELS = 2
HIGHEST = lax.Precision.HIGHEST
VMEM_LIMIT = 20 * 1024 * 1024

def spread(row):
    return jnp.broadcast_to(row, (8, row.shape[1]))


def lane(tile, k):
    return jnp.broadcast_to(tile[:, k:k + 1], (8, 128))


def factor_tile(matrix, tasks=()):
    groups = 16
    rows_of = lax.broadcasted_iota(jnp.int32, (8, 128), 0)
    cols_of = lax.broadcasted_iota(jnp.int32, (8, 128), 1)
    left = [matrix[8 * g:8 * g + 8, :] for g in range(groups)]
    right = [(cols_of == rows_of + 8 * g).astype(jnp.float32) for g in range(groups)]
    upper, inverse = [], []
    for s in range(groups):
        y = [spread(left[s][k:k + 1, :]) for k in range(8)]
        v = [spread(right[s][k:k + 1, :]) for k in range(8)]
        d = [[lane(y[i], 8 * s + k) if k >= i else None for k in range(8)] for i in range(8)]
        last = s + 1 == groups
        columns = [[lane(left[g], 8 * s + k) for k in range(8)] for g in range(s + 1, groups)]
        e = list(columns[0]) if not last else None
        ratio = [[None] * 8 for _ in range(8)]
        inv = []
        for k in range(8):
            inv.append(pl.reciprocal(d[k][k], approx=True))
            for i in range(k + 1, 8):
                ratio[i][k] = d[k][i] * inv[k]
                for j in range(i, 8):
                    d[i][j] = d[i][j] - ratio[i][k] * d[k][j]
                y[i] = y[i] - ratio[i][k] * y[k]
                v[i] = v[i] - ratio[i][k] * v[k]
            if not last:
                left[s + 1] = left[s + 1] - e[k] * inv[k] * y[k]
                for j in range(k + 1, 8):
                    e[j] = e[j] - e[k] * ratio[j][k]
        up = jnp.zeros((8, 128), jnp.float32)
        low = jnp.zeros((8, 128), jnp.float32)
        for k in range(8):
            root = lax.rsqrt(d[k][k])
            up = jnp.where(rows_of == k, y[k] * root, up)
            low = jnp.where(rows_of == k, v[k] * root, low)
        upper.append(jnp.where(cols_of >= rows_of + 8 * s, up, 0.0))
        inverse.append(low)
        if s < len(tasks):
            tasks[s]()
        if last:
            break
        x, w = [None] * 8, [None] * 8
        for k in reversed(range(8)):
            x[k] = y[k] * inv[k]
            w[k] = v[k] * inv[k]
            for j in reversed(range(k + 1, 8)):
                x[k] = x[k] - ratio[j][k] * x[j]
                w[k] = w[k] - ratio[j][k] * w[j]
        for g in range(s + 1, groups):
            f = columns[g - s - 1]
            for k in reversed(range(8)):
                if g > s + 1:
                    left[g] = left[g] - f[k] * x[k]
                right[g] = right[g] - f[k] * w[k]
    return jnp.concatenate(upper, axis=0), jnp.concatenate(inverse, axis=0)


def dot(a, b, dims=((1,), (0,))):
    return lax.dot_general(a, b, (dims, ((), ())), precision=HIGHEST, preferred_element_type=jnp.float32)

ROWS = ((1,), (1,))

def mul(a, b, dims=((1,), (0,))):
    return lax.dot_general(a, b, (dims, ((), ())), preferred_element_type=jnp.float32)


def split(x):
    pieces = []
    for _ in range(3):
        pieces.append(x.astype(jnp.bfloat16))
        x = x - pieces[-1].astype(jnp.float32)
    return pieces


def product(pieces, block):
    return sum(mul(pieces[p], block) for p in (2, 1, 0))


def solve(rows, pieces):
    return sum(mul(rows, pieces[p], ROWS) for p in (2, 1, 0))


def factor_rest(upper_1, inv_1, side, rest, lower_ref, pieces_ref, tasks=()):
    half = side.shape[0]
    pieces = split(inv_1)
    lower_21 = solve(side, pieces)
    rest = rest.astype(jnp.float32) - dot(lower_21, lower_21, ROWS)
    beside = dot(lower_21, inv_1)

    def store_left():
        lower_ref[half:, :half] = lower_21
        lower_ref[:half, half:] = jnp.zeros((half, half), jnp.float32)
        lower_ref[:half, :half] = upper_1.T

    def store_pieces():
        for p in range(3):
            pieces_ref[p, :half, :half] = pieces[p]
            pieces_ref[p, :half, half:] = jnp.zeros((half, half), jnp.bfloat16)

    upper_2, inv_2 = factor_tile(rest, [store_left, store_pieces] + list(tasks))
    inv_21 = -dot(inv_2, beside)
    lower_ref[half:, half:] = upper_2.T
    for p, (left, right) in enumerate(zip(split(inv_21), split(inv_2))):
        pieces_ref[p, half:, :half] = left
        pieces_ref[p, half:, half:] = right


def start_kernel(quarter_ref, upper_ref, inverse_ref):
    upper, inverse = factor_tile(quarter_ref[...].astype(jnp.float32))
    upper_ref[...] = upper
    inverse_ref[...] = inverse


def first_kernel(rest_ref, upper_ref, tile_inverse_ref, lower_ref, pieces_ref):
    half = rest_ref.shape[1]
    factor_rest(upper_ref[...], tile_inverse_ref[...], rest_ref[:half], rest_ref[half:], lower_ref, pieces_ref)


def second_start_kernel(
    top_10_ref, rest_10_ref, rest_01_ref, top_11_ref, rest_11_ref, pieces_0_ref,
    panel_ref, later_ref, upper_ref, inverse_ref,
):
    half = top_11_ref.shape[1]
    corner = rest_01_ref[:half].astype(jnp.float32).T.astype(jnp.bfloat16)
    left = jnp.concatenate([top_10_ref[...], rest_10_ref[:half]], axis=0)
    right = jnp.concatenate([corner, rest_10_ref[half:]], axis=0)
    panel = solve(jnp.concatenate([left, right], axis=1), pieces_0_ref).astype(jnp.bfloat16)
    above, below = panel[:half], panel[half:]
    top = (top_11_ref[...].astype(jnp.float32) - mul(above, above, ROWS)).astype(jnp.bfloat16)

    def side():
        panel_ref[...] = panel
        later_ref[:half] = (rest_11_ref[:half].astype(jnp.float32) - mul(below, above, ROWS)).astype(jnp.bfloat16)

    def rest():
        later_ref[half:] = (rest_11_ref[half:].astype(jnp.float32) - mul(below, below, ROWS)).astype(jnp.bfloat16)

    upper, inverse = factor_tile(top.astype(jnp.float32), (side, rest))
    upper_ref[...] = upper
    inverse_ref[...] = inverse


def second_kernel(
    rest_ref, upper_ref, tile_inverse_ref, pieces_0_ref, panel_ref, above_0_ref, above_1_ref,
    lower_ref, pieces_1_ref, mirror_ref, later_ref,
):
    half = rest_ref.shape[1]
    tasks = []
    for m in range(above_0_ref.shape[0]):
        for part in (pl.ds(0, half), pl.ds(half, half)):
            def mirror(m=m, part=part):
                mirror_ref[m, part] = sum(mul(pieces_0_ref[p, part], above_0_ref[m]) for p in (2, 1, 0)).astype(jnp.bfloat16)
            tasks.append(mirror)
    for m in range(above_0_ref.shape[0]):
        for part in (pl.ds(0, half), pl.ds(half, half)):
            def later(m=m, part=part):
                change = mul(panel_ref[part], mirror_ref[m])
                later_ref[m, part] = (above_1_ref[m, part].astype(jnp.float32) - change).astype(jnp.bfloat16)
            tasks.append(later)
    factor_rest(
        upper_ref[...], tile_inverse_ref[...], rest_ref[:half], rest_ref[half:], lower_ref, pieces_1_ref, tasks)


def update_kernel(
    ids_ref, column_0_ref, column_1_ref, blocks_ref, mirror_0_ref, later_ref,
    lower_0_ref, lower_1_ref, pieces_0_ref, pieces_1_ref, panel_10_ref,
    panels_ref, schur_ref, mirror_1_ref,
):
    step = pl.program_id(0)
    batch, col_blocks, width = blocks_ref.shape[:3]

    @pl.when(step == 0)
    def _():
        for m in range(col_blocks):
            mirror_1_ref[m] = product(pieces_1_ref, later_ref[m]).astype(jnp.bfloat16)

    ids = [(step * batch + i) * ids_ref[2] + ids_ref[0] for i in range(batch)]

    def below(solved, panel, lower_ref):
        parts = []
        for i, block_row in enumerate(ids):
            part = jnp.where(block_row > panel, solved[i * width:(i + 1) * width], 0.0)
            panels_ref[i, panel] = jnp.where(block_row == panel, lower_ref[...], part)
            parts.append(part)
        return jnp.concatenate(parts, axis=0).astype(jnp.bfloat16)

    rounded_0 = below(solve(column_0_ref[...].reshape(batch * width, width), pieces_0_ref), 0, lower_0_ref)
    column = column_1_ref[...].reshape(batch * width, width).astype(jnp.float32)
    column = (column - mul(rounded_0, panel_10_ref[...], ROWS)).astype(jnp.bfloat16)
    rounded_1 = below(solve(column, pieces_1_ref), 1, lower_1_ref)
    for m in range(col_blocks):
        change_0 = mul(rounded_0, mirror_0_ref[m])
        change_1 = mul(rounded_1, mirror_1_ref[m])
        for i, block_row in enumerate(ids):
            part = slice(i * width, (i + 1) * width)
            block = blocks_ref[i, m].astype(jnp.float32) - change_0[part]
            block = block.astype(jnp.bfloat16).astype(jnp.float32) - change_1[part]
            keep = (block_row >= PANELS) & (m * ids_ref[3] + ids_ref[1] >= PANELS)
            schur_ref[i, m] = jnp.where(keep, block, 0.0).astype(jnp.bfloat16)


FACTOR_COST = pl.CostEstimate(flops=10**6, bytes_accessed=10**4, transcendentals=0)


def call_factor(kernel, name, shapes, *operands):
    return pl.pallas_call(
        kernel, out_shape=shapes, name=name, cost_estimate=FACTOR_COST,
        compiler_params=pltpu.CompilerParams(vmem_limit_bytes=VMEM_LIMIT),
    )(*operands)


def square(width, dtype=jnp.float32):
    return jax.ShapeDtypeStruct((width, width), dtype)


def update(ids, column_0, column_1, blocks, mirror_0, later, lower_0, lower_1, pieces_0, pieces_1, panel_10):
    row_blocks, col_blocks, width = blocks.shape[:3]
    batch = 2 if row_blocks % 2 == 0 else 1
    rows_spec = pl.BlockSpec((batch, width, width), lambda i: (i, 0, 0))
    square_spec = pl.BlockSpec((width, width), lambda i: (0, 0))
    mirror_spec = pl.BlockSpec((col_blocks, width, width), lambda i: (0, 0, 0))
    pieces_spec = pl.BlockSpec((3, width, width), lambda i: (0, 0, 0))
    block_spec = pl.BlockSpec((batch, col_blocks, width, width), lambda i: (i, 0, 0, 0))
    return pl.pallas_call(
        update_kernel,
        grid=(row_blocks // batch,),
        in_specs=[pl.BlockSpec(memory_space=pltpu.SMEM), rows_spec, rows_spec, block_spec, mirror_spec, mirror_spec]
        + [square_spec] * 2 + [pieces_spec] * 2 + [square_spec],
        out_specs=[pl.BlockSpec((batch, PANELS, width, width), lambda i: (i, 0, 0, 0)), block_spec],
        out_shape=[
            jax.ShapeDtypeStruct((row_blocks, PANELS, width, width), jnp.float32),
            jax.ShapeDtypeStruct(blocks.shape, jnp.bfloat16),
        ],
        scratch_shapes=[pltpu.VMEM((col_blocks, width, width), jnp.bfloat16)],
        compiler_params=pltpu.CompilerParams(vmem_limit_bytes=VMEM_LIMIT),
        cost_estimate=pl.CostEstimate(flops=2 * 10**9, bytes_accessed=6 * 10**6, transcendentals=0),
        name="solve_and_update",
    )(ids, column_0, column_1, blocks, mirror_0, later, lower_0, lower_1, pieces_0, pieces_1, panel_10)


def pack_kernel(kernel_ref, quarters_ref, semaphores):
    half = quarters_ref.shape[1]
    copies = []
    for q, (row, col) in enumerate(((0, 0), (1, 0), (1, 1))):
        source = kernel_ref.at[0, 0, 0, 0, pl.ds(row * half, half), pl.ds(col * half, half)]
        copies.append(pltpu.make_async_copy(source, quarters_ref.at[pl.ds(q * half, half)], semaphores.at[q]))
    for copy in copies:
        copy.start()
    for copy in copies:
        copy.wait()


def pack(kernel):
    half = kernel.shape[-1] // 2
    return pl.pallas_call(
        pack_kernel,
        in_specs=[pl.BlockSpec(memory_space=pltpu.HBM)],
        out_shape=jax.ShapeDtypeStruct((3 * half, half), kernel.dtype),
        scratch_shapes=[pltpu.SemaphoreType.DMA((3,))],
        compiler_params=pltpu.CompilerParams(vmem_limit_bytes=2 * 1024 * 1024),
        name="pack",
    )(kernel)


def swap(block, axis, distance):
    count = lax.axis_size(axis)
    return lax.ppermute(block, axis, [(d, d ^ distance) for d in range(count)])


HOLDERS = ((0, 0), (0, 1), (1, 0), (1, 1))


def diagonal_along(quarters, my_col):
    col_count = lax.axis_size("col")
    along = quarters
    for chip in range(1, col_count // 2):
        pairs = [(r * col_count + core, r * col_count + chip * 2 + core) for r, core in HOLDERS]
        got = lax.ppermute(quarters, ("row", "col"), pairs)
        along = jnp.where(my_col // 2 == chip, got, along)
    return along


def diagonal_down(along, my_row):
    first, second = along, along
    for step in range(1, lax.axis_size("row")):
        got = swap(along, "row", step)
        first = jnp.where(my_row == step, got, first)
        second = jnp.where(my_row == step ^ 1, got, second)
    return jnp.stack([first, second])


def both_cores(pair, my_col):
    other = swap(pair, "col", 1)
    even = my_col % 2 == 0
    left = jnp.where(even, pair, other)
    right = jnp.where(even, other, pair)
    return left[0], right[0], left[1], right[1]


def first_reach(block):
    return block, swap(block, "row", 2)


def other_reaches(block, got, my_row):
    reach = 2
    while True:
        block = jnp.where((my_row >= reach) & (my_row < 2 * reach), got, block)
        reach *= 2
        if reach >= lax.axis_size("row"):
            return block
        got = swap(block, "row", reach)


def by_row(block, other, my_row):
    even = my_row % 2 == 0
    return jnp.where(even, block, other), jnp.where(even, other, block)


def first_stride(block):
    chips = lax.axis_size("col") // 2
    pairs = [(core, core + chips) for core in range(2)]
    return block, lax.ppermute(block, "col", pairs)


def other_strides(block, got, my_col):
    chips = lax.axis_size("col") // 2
    stride = chips // 2
    while True:
        block = jnp.where((my_col // 2) % (2 * stride) == stride, got, block)
        stride //= 2
        if stride == 0:
            return block
        if stride == 1:
            got = swap(block, "col", 2)
        else:
            sources = [chip * 2 + core for chip in range(0, chips, 2 * stride) for core in range(2)]
            got = lax.ppermute(block, "col", [(s, s + 2 * stride) for s in sources])


def per_device(kernel):
    my_row = lax.axis_index("row")
    my_col = lax.axis_index("col")
    even = my_col % 2 == 0
    blocks = kernel[0, :, 0]
    col_blocks, width = blocks.shape[1:3]
    half = width // 2
    quarters = pack(kernel)
    rows, above, _ = lax.optimization_barrier((blocks[:, 0], blocks[0], quarters))
    rows, rows_got = first_stride(rows)
    above, above_got = first_reach(above)
    along = diagonal_along(quarters, my_col)
    pair = diagonal_down(along, my_row)
    pair, rows, rows_got = lax.optimization_barrier((pair, rows, rows_got))
    block_00, block_01, block_10, block_11 = both_cores(pair, my_col)
    rows = other_strides(rows, rows_got, my_col)
    upper_0, tile_inverse_0 = call_factor(start_kernel, "factor_start", [square(half)] * 2, block_00[:half])
    above, above_got, tile_inverse_0 = lax.optimization_barrier((above, above_got, tile_inverse_0))
    above = other_reaches(above, above_got, my_row)
    above_other = swap(above, "row", 1)
    pieces = jax.ShapeDtypeStruct((3, width, width), jnp.bfloat16)
    lower_0, pieces_0 = call_factor(
        first_kernel, "factor_first", [square(width), pieces], block_00[half:], upper_0, tile_inverse_0)
    panel_10, rest_11, upper_1, tile_inverse_1 = call_factor(
        second_start_kernel, "factor_second_start",
        [square(width, jnp.bfloat16), jax.ShapeDtypeStruct((width, half), jnp.bfloat16), square(half), square(half)],
        block_10[:half], block_10[half:], block_01[half:], block_11[:half], block_11[half:], pieces_0)
    rows, above, above_other, tile_inverse_1 = lax.optimization_barrier((rows, above, above_other, tile_inverse_1))
    above_0, above_1 = by_row(above, above_other, my_row)
    other = swap(rows, "col", 1)
    mirror = jax.ShapeDtypeStruct((col_blocks, width, width), jnp.bfloat16)
    lower_1, pieces_1, mirror_0, later = call_factor(
        second_kernel, "factor_second", [square(width), pieces, mirror, mirror],
        rest_11, upper_1, tile_inverse_1, pieces_0, panel_10, above_0, above_1)
    other, lower_1 = lax.optimization_barrier((other, lower_1))
    column_0 = jnp.where(even, rows, other)
    column_1 = jnp.where(even, other, rows)
    ids = jnp.stack([my_row, my_col, lax.axis_size("row"), lax.axis_size("col")]).astype(jnp.int32)
    panels, schur = update(
        ids, column_0, column_1, blocks, mirror_0, later, lower_0, lower_1, pieces_0, pieces_1, panel_10)
    return (panels[None], schur[None, :, None])


def solution(mesh):
    in_specs = (P("row", None, "col", None, None, None),)
    out_specs = (P("row", None, None, None, None), P("row", None, "col", None, None, None))
    return jax.shard_map(
        per_device, mesh=mesh, in_specs=in_specs, out_specs=out_specs, check_vma=False
    )
```

```python
import jax
import jax.numpy as jnp
from jax import lax
from jax.experimental import pallas as pl
from jax.experimental.pallas import tpu as pltpu
from jax.sharding import PartitionSpec as P

PANELS = 2
HIGHEST = lax.Precision.HIGHEST
VMEM_LIMIT = 20 * 1024 * 1024

def spread(row):
    return jnp.broadcast_to(row, (8, row.shape[1]))


def lane(tile, k):
    return jnp.broadcast_to(tile[:, k:k + 1], (8, 128))


def factor_tile(matrix, tasks=()):
    groups = 16
    rows_of = lax.broadcasted_iota(jnp.int32, (8, 128), 0)
    cols_of = lax.broadcasted_iota(jnp.int32, (8, 128), 1)
    left = [matrix[8 * g:8 * g + 8, :] for g in range(groups)]
    right = [(cols_of == rows_of + 8 * g).astype(jnp.float32) for g in range(groups)]
    upper, inverse = [], []
    for s in range(groups):
        y = [spread(left[s][k:k + 1, :]) for k in range(8)]
        v = [spread(right[s][k:k + 1, :]) for k in range(8)]
        d = [[lane(y[i], 8 * s + k) if k >= i else None for k in range(8)] for i in range(8)]
        last = s + 1 == groups
        near = None if last else [lane(left[s + 1], 8 * s + k) for k in range(8)]
        e = None if last else list(near)
        ratio = [[None] * 8 for _ in range(8)]
        inv = []
        for k in range(8):
            inv.append(pl.reciprocal(d[k][k], approx=True))
            for i in range(k + 1, 8):
                ratio[i][k] = d[k][i] * inv[k]
                for j in range(i, 8):
                    d[i][j] = d[i][j] - ratio[i][k] * d[k][j]
                y[i] = y[i] - ratio[i][k] * y[k]
                v[i] = v[i] - ratio[i][k] * v[k]
            if not last:
                left[s + 1] = left[s + 1] - e[k] * inv[k] * y[k]
                for j in range(k + 1, 8):
                    e[j] = e[j] - e[k] * ratio[j][k]
        up = jnp.zeros((8, 128), jnp.float32)
        low = jnp.zeros((8, 128), jnp.float32)
        for k in range(8):
            root = lax.rsqrt(d[k][k])
            up = jnp.where(rows_of == k, y[k] * root, up)
            low = jnp.where(rows_of == k, v[k] * root, low)
        upper.append(jnp.where(cols_of >= rows_of + 8 * s, up, 0.0))
        inverse.append(low)
        if s < len(tasks):
            tasks[s]()
        if last:
            break
        x, w = [None] * 8, [None] * 8
        for k in reversed(range(8)):
            x[k] = y[k] * inv[k]
            w[k] = v[k] * inv[k]
            for j in reversed(range(k + 1, 8)):
                x[k] = x[k] - ratio[j][k] * x[j]
                w[k] = w[k] - ratio[j][k] * w[j]
        for g in range(s + 1, groups):
            f = near if g == s + 1 else [lane(left[g], 8 * s + k) for k in range(8)]
            for k in reversed(range(8)):
                if g > s + 1:
                    left[g] = left[g] - f[k] * x[k]
                right[g] = right[g] - f[k] * w[k]
    return jnp.concatenate(upper, axis=0), jnp.concatenate(inverse, axis=0)


def dot(a, b, dims=((1,), (0,))):
    return lax.dot_general(a, b, (dims, ((), ())), precision=HIGHEST, preferred_element_type=jnp.float32)

ROWS = ((1,), (1,))

def mul(a, b, dims=((1,), (0,))):
    return lax.dot_general(a, b, (dims, ((), ())), preferred_element_type=jnp.float32)


def split(x):
    pieces = []
    for _ in range(3):
        pieces.append(x.astype(jnp.bfloat16))
        x = x - pieces[-1].astype(jnp.float32)
    return pieces


def product(pieces, block):
    return sum(mul(pieces[p], block) for p in (2, 1, 0))


def solve(rows, pieces):
    return sum(mul(rows, pieces[p], ROWS) for p in (2, 1, 0))


def factor_rest(upper_1, inv_1, side, rest, lower_ref, pieces_ref, tasks=()):
    half = side.shape[0]
    pieces = split(inv_1)
    lower_21 = solve(side, pieces)
    rest = rest.astype(jnp.float32) - dot(lower_21, lower_21, ROWS)
    beside = dot(lower_21, inv_1)

    def store_left():
        lower_ref[half:, :half] = lower_21
        lower_ref[:half, half:] = jnp.zeros((half, half), jnp.float32)
        lower_ref[:half, :half] = upper_1.T

    def store_pieces():
        for p in range(3):
            pieces_ref[p, :half, :half] = pieces[p]
            pieces_ref[p, :half, half:] = jnp.zeros((half, half), jnp.bfloat16)

    upper_2, inv_2 = factor_tile(rest, [store_left, store_pieces] + list(tasks))
    inv_21 = -dot(inv_2, beside)
    lower_ref[half:, half:] = upper_2.T
    for p, (left, right) in enumerate(zip(split(inv_21), split(inv_2))):
        pieces_ref[p, half:, :half] = left
        pieces_ref[p, half:, half:] = right


def start_kernel(quarter_ref, upper_ref, inverse_ref):
    upper, inverse = factor_tile(quarter_ref[...].astype(jnp.float32))
    upper_ref[...] = upper
    inverse_ref[...] = inverse


def first_kernel(rest_ref, upper_ref, tile_inverse_ref, lower_ref, pieces_ref):
    half = rest_ref.shape[1]
    factor_rest(upper_ref[...], tile_inverse_ref[...], rest_ref[:half], rest_ref[half:], lower_ref, pieces_ref)


def second_start_kernel(
    top_10_ref, rest_10_ref, rest_01_ref, top_11_ref, rest_11_ref, pieces_0_ref,
    panel_ref, later_ref, upper_ref, inverse_ref,
):
    half = top_11_ref.shape[1]
    corner = rest_01_ref[:half].astype(jnp.float32).T.astype(jnp.bfloat16)
    left = jnp.concatenate([top_10_ref[...], rest_10_ref[:half]], axis=0)
    right = jnp.concatenate([corner, rest_10_ref[half:]], axis=0)
    panel = solve(jnp.concatenate([left, right], axis=1), pieces_0_ref).astype(jnp.bfloat16)
    above, below = panel[:half], panel[half:]
    top = (top_11_ref[...].astype(jnp.float32) - mul(above, above, ROWS)).astype(jnp.bfloat16)

    def side():
        panel_ref[...] = panel
        later_ref[:half] = (rest_11_ref[:half].astype(jnp.float32) - mul(below, above, ROWS)).astype(jnp.bfloat16)

    def rest():
        later_ref[half:] = (rest_11_ref[half:].astype(jnp.float32) - mul(below, below, ROWS)).astype(jnp.bfloat16)

    upper, inverse = factor_tile(top.astype(jnp.float32), (side, rest))
    upper_ref[...] = upper
    inverse_ref[...] = inverse


def second_kernel(
    ids_ref, rest_ref, upper_ref, tile_inverse_ref, pieces_0_ref, panel_ref, above_ref, other_ref,
    lower_ref, pieces_1_ref, mirror_ref, later_ref,
):
    half = rest_ref.shape[1]
    even = ids_ref[0] % 2 == 0
    tasks = []
    for m in range(above_ref.shape[0]):
        def mirror(m=m):
            above = jnp.where(even, above_ref[m], other_ref[m])
            mirror_ref[m] = product(pieces_0_ref, above).astype(jnp.bfloat16)

        def later(m=m):
            above = jnp.where(even, other_ref[m], above_ref[m]).astype(jnp.float32)
            later_ref[m] = (above - mul(panel_ref[...], mirror_ref[m])).astype(jnp.bfloat16)

        tasks += [mirror, later]
    factor_rest(
        upper_ref[...], tile_inverse_ref[...], rest_ref[:half], rest_ref[half:], lower_ref, pieces_1_ref, tasks)


def update_kernel(
    ids_ref, column_0_ref, column_1_ref, blocks_ref, mirror_0_ref, later_ref,
    lower_0_ref, lower_1_ref, pieces_0_ref, pieces_1_ref, panel_10_ref,
    panels_ref, schur_ref, panels_here, schur_here, mirror_1_ref, panels_done, schur_done,
):
    row_blocks, col_blocks, width = blocks_ref.shape[:3]
    size = 2 if row_blocks % 2 == 0 else 1
    batches = range(0, row_blocks, size)
    ids = [i * ids_ref[2] + ids_ref[0] for i in range(row_blocks)]
    copies = []

    def send(source, target, semaphore):
        copies.append(pltpu.make_async_copy(source, target, semaphore))
        copies[-1].start()

    def below(solved, panel, lower_ref, start):
        parts = []
        for i in range(start, start + size):
            part = jnp.where(ids[i] > panel, solved[(i - start) * width:(i - start + 1) * width], 0.0)
            panels_here[i, panel] = jnp.where(ids[i] == panel, lower_ref[...], part)
            send(panels_here.at[i, panel], panels_ref.at[i, panel], panels_done.at[i, panel])
            parts.append(part)
        return jnp.concatenate(parts, axis=0).astype(jnp.bfloat16)

    def batch(column_ref, start):
        return column_ref[start:start + size].reshape(size * width, width)

    rounded_0 = [below(solve(batch(column_0_ref, b), pieces_0_ref), 0, lower_0_ref, b) for b in batches]
    columns = []
    for b, rounded in zip(batches, rounded_0):
        change = mul(rounded, panel_10_ref[...], ROWS)
        columns.append((batch(column_1_ref, b).astype(jnp.float32) - change).astype(jnp.bfloat16))
    for m in range(col_blocks):
        mirror_1_ref[m] = product(pieces_1_ref, later_ref[m]).astype(jnp.bfloat16)
    rounded_1 = [below(solve(column, pieces_1_ref), 1, lower_1_ref, b) for b, column in zip(batches, columns)]
    for b, left_0, left_1 in zip(batches, rounded_0, rounded_1):
        for m in range(col_blocks):
            change_0 = mul(left_0, mirror_0_ref[m])
            change_1 = mul(left_1, mirror_1_ref[m])
            for i in range(b, b + size):
                part = slice((i - b) * width, (i - b + 1) * width)
                block = blocks_ref[i, m].astype(jnp.float32) - change_0[part]
                block = block.astype(jnp.bfloat16).astype(jnp.float32) - change_1[part]
                keep = (ids[i] >= PANELS) & (m * ids_ref[3] + ids_ref[1] >= PANELS)
                schur_here[i, m] = jnp.where(keep, block, 0.0).astype(jnp.bfloat16)
        for i in range(b, b + size):
            send(schur_here.at[i], schur_ref.at[i], schur_done.at[i])
    for copy in copies:
        copy.wait()


FACTOR_COST = pl.CostEstimate(flops=10**6, bytes_accessed=10**4, transcendentals=0)


def call_factor(kernel, name, shapes, *operands):
    in_specs = [
        pl.BlockSpec(memory_space=pltpu.SMEM if x.dtype == jnp.int32 else pltpu.VMEM) for x in operands]
    return pl.pallas_call(
        kernel, in_specs=in_specs, out_shape=shapes, name=name, cost_estimate=FACTOR_COST,
        compiler_params=pltpu.CompilerParams(vmem_limit_bytes=VMEM_LIMIT),
    )(*operands)


def square(width, dtype=jnp.float32):
    return jax.ShapeDtypeStruct((width, width), dtype)


def update(ids, column_0, column_1, blocks, mirror_0, later, lower_0, lower_1, pieces_0, pieces_1, panel_10):
    row_blocks, col_blocks, width = blocks.shape[:3]
    panels = jax.ShapeDtypeStruct((row_blocks, PANELS, width, width), jnp.float32)
    schur = jax.ShapeDtypeStruct(blocks.shape, jnp.bfloat16)
    return pl.pallas_call(
        update_kernel,
        in_specs=[pl.BlockSpec(memory_space=pltpu.SMEM)] + [pl.BlockSpec(memory_space=pltpu.VMEM)] * 10,
        out_specs=[pl.BlockSpec(memory_space=pl.ANY)] * 2,
        out_shape=[panels, schur],
        scratch_shapes=[
            pltpu.VMEM(panels.shape, panels.dtype),
            pltpu.VMEM(schur.shape, schur.dtype),
            pltpu.VMEM((col_blocks, width, width), jnp.bfloat16),
            pltpu.SemaphoreType.DMA((row_blocks, PANELS)),
            pltpu.SemaphoreType.DMA((row_blocks,)),
        ],
        compiler_params=pltpu.CompilerParams(vmem_limit_bytes=VMEM_LIMIT),
        cost_estimate=pl.CostEstimate(flops=2 * 10**9, bytes_accessed=6 * 10**6, transcendentals=0),
        name="solve_and_update",
    )(ids, column_0, column_1, blocks, mirror_0, later, lower_0, lower_1, pieces_0, pieces_1, panel_10)


def pack_kernel(kernel_ref, quarters_ref, semaphores):
    half = quarters_ref.shape[1]
    copies = []
    for q, (row, col) in enumerate(((0, 0), (1, 0), (1, 1))):
        source = kernel_ref.at[0, 0, 0, 0, pl.ds(row * half, half), pl.ds(col * half, half)]
        copies.append(pltpu.make_async_copy(source, quarters_ref.at[pl.ds(q * half, half)], semaphores.at[q]))
    for copy in copies:
        copy.start()
    for copy in copies:
        copy.wait()


def pack(kernel):
    half = kernel.shape[-1] // 2
    return pl.pallas_call(
        pack_kernel,
        in_specs=[pl.BlockSpec(memory_space=pltpu.HBM)],
        out_shape=jax.ShapeDtypeStruct((3 * half, half), kernel.dtype),
        scratch_shapes=[pltpu.SemaphoreType.DMA((3,))],
        compiler_params=pltpu.CompilerParams(vmem_limit_bytes=2 * 1024 * 1024),
        name="pack",
    )(kernel)


def swap(block, axis, distance):
    count = lax.axis_size(axis)
    return lax.ppermute(block, axis, [(d, d ^ distance) for d in range(count)])


HOLDERS = ((0, 0), (0, 1), (1, 0), (1, 1))


def diagonal_along(quarters, my_col):
    col_count = lax.axis_size("col")
    along = quarters
    for chip in range(1, col_count // 2):
        pairs = [(r * col_count + core, r * col_count + chip * 2 + core) for r, core in HOLDERS]
        got = lax.ppermute(quarters, ("row", "col"), pairs)
        along = jnp.where(my_col // 2 == chip, got, along)
    return along


def diagonal_down(along, my_row):
    first, second = along, along
    for step in range(1, lax.axis_size("row")):
        got = swap(along, "row", step)
        first = jnp.where(my_row == step, got, first)
        second = jnp.where(my_row == step ^ 1, got, second)
    return jnp.stack([first, second])


def both_cores(pair, my_col):
    other = swap(pair, "col", 1)
    even = my_col % 2 == 0
    left = jnp.where(even, pair, other)
    right = jnp.where(even, other, pair)
    return left[0], right[0], left[1], right[1]


def first_reach(block):
    return block, swap(block, "row", 2)


def other_reaches(block, got, my_row):
    reach = 2
    while True:
        block = jnp.where((my_row >= reach) & (my_row < 2 * reach), got, block)
        reach *= 2
        if reach >= lax.axis_size("row"):
            return block
        got = swap(block, "row", reach)


def first_stride(block):
    chips = lax.axis_size("col") // 2
    pairs = [(core, core + chips) for core in range(2)]
    return block, lax.ppermute(block, "col", pairs)


def other_strides(block, got, my_col):
    chips = lax.axis_size("col") // 2
    stride = chips // 2
    while True:
        block = jnp.where((my_col // 2) % (2 * stride) == stride, got, block)
        stride //= 2
        if stride == 0:
            return block
        if stride == 1:
            got = swap(block, "col", 2)
        else:
            sources = [chip * 2 + core for chip in range(0, chips, 2 * stride) for core in range(2)]
            got = lax.ppermute(block, "col", [(s, s + 2 * stride) for s in sources])


def per_device(kernel):
    my_row = lax.axis_index("row")
    my_col = lax.axis_index("col")
    even = my_col % 2 == 0
    blocks = kernel[0, :, 0]
    col_blocks, width = blocks.shape[1:3]
    half = width // 2
    ids = jnp.stack([my_row, my_col, lax.axis_size("row"), lax.axis_size("col")]).astype(jnp.int32)
    quarters = pack(kernel)
    rows, above, _ = lax.optimization_barrier((blocks[:, 0], blocks[0], quarters))
    rows, rows_got = first_stride(rows)
    above, above_got = first_reach(above)
    along = diagonal_along(quarters, my_col)
    pair = diagonal_down(along, my_row)
    pair, rows, rows_got = lax.optimization_barrier((pair, rows, rows_got))
    block_00, block_01, block_10, block_11 = both_cores(pair, my_col)
    rows = other_strides(rows, rows_got, my_col)
    upper_0, tile_inverse_0 = call_factor(start_kernel, "factor_start", [square(half)] * 2, block_00[:half])
    above, above_got, tile_inverse_0 = lax.optimization_barrier((above, above_got, tile_inverse_0))
    above = other_reaches(above, above_got, my_row)
    above_other = swap(above, "row", 1)
    pieces = jax.ShapeDtypeStruct((3, width, width), jnp.bfloat16)
    lower_0, pieces_0 = call_factor(
        first_kernel, "factor_first", [square(width), pieces], block_00[half:], upper_0, tile_inverse_0)
    panel_10, rest_11, upper_1, tile_inverse_1 = call_factor(
        second_start_kernel, "factor_second_start",
        [square(width, jnp.bfloat16), jax.ShapeDtypeStruct((width, half), jnp.bfloat16), square(half), square(half)],
        block_10[:half], block_10[half:], block_01[half:], block_11[:half], block_11[half:], pieces_0)
    rows, above, above_other, tile_inverse_1 = lax.optimization_barrier((rows, above, above_other, tile_inverse_1))
    other = swap(rows, "col", 1)
    mirror = jax.ShapeDtypeStruct((col_blocks, width, width), jnp.bfloat16)
    lower_1, pieces_1, mirror_0, later = call_factor(
        second_kernel, "factor_second", [square(width), pieces, mirror, mirror],
        ids, rest_11, upper_1, tile_inverse_1, pieces_0, panel_10, above, above_other)
    other, lower_1 = lax.optimization_barrier((other, lower_1))
    column_0 = jnp.where(even, rows, other)
    column_1 = jnp.where(even, other, rows)
    panels, schur = update(
        ids, column_0, column_1, blocks, mirror_0, later, lower_0, lower_1, pieces_0, pieces_1, panel_10)
    return (panels[None], schur[None, :, None])


def solution(mesh):
    in_specs = (P("row", None, "col", None, None, None),)
    out_specs = (P("row", None, None, None, None), P("row", None, "col", None, None, None))
    return jax.shard_map(
        per_device, mesh=mesh, in_specs=in_specs, out_specs=out_specs, check_vma=False
    )
```

```python
import jax
import jax.numpy as jnp
from jax import lax
from jax.experimental import pallas as pl
from jax.experimental.pallas import tpu as pltpu
from jax.sharding import PartitionSpec as P

PANELS = 2
HIGHEST = lax.Precision.HIGHEST
VMEM_LIMIT = 20 * 1024 * 1024

def spread(row):
    return jnp.broadcast_to(row, (8, row.shape[1]))


def lane(tile, k):
    return jnp.broadcast_to(tile[:, k:k + 1], (8, 128))


def factor_tile(matrix, tasks=()):
    groups = 16
    rows_of = lax.broadcasted_iota(jnp.int32, (8, 128), 0)
    cols_of = lax.broadcasted_iota(jnp.int32, (8, 128), 1)
    left = [matrix[8 * g:8 * g + 8, :] for g in range(groups)]
    right = [(cols_of == rows_of + 8 * g).astype(jnp.float32) for g in range(groups)]
    upper, inverse = [], []
    for s in range(groups):
        y = [spread(left[s][k:k + 1, :]) for k in range(8)]
        v = [spread(right[s][k:k + 1, :]) for k in range(8)]
        d = [[lane(y[i], 8 * s + k) if k >= i else None for k in range(8)] for i in range(8)]
        last = s + 1 == groups
        near = None if last else [lane(left[s + 1], 8 * s + k) for k in range(8)]
        e = None if last else list(near)
        ratio = [[None] * 8 for _ in range(8)]
        inv = []
        for k in range(8):
            inv.append(pl.reciprocal(d[k][k], approx=True))
            for i in range(k + 1, 8):
                ratio[i][k] = d[k][i] * inv[k]
                for j in range(i, 8):
                    d[i][j] = d[i][j] - ratio[i][k] * d[k][j]
                y[i] = y[i] - ratio[i][k] * y[k]
                v[i] = v[i] - ratio[i][k] * v[k]
            if not last:
                left[s + 1] = left[s + 1] - e[k] * inv[k] * y[k]
                for j in range(k + 1, 8):
                    e[j] = e[j] - e[k] * ratio[j][k]
        up = jnp.zeros((8, 128), jnp.float32)
        low = jnp.zeros((8, 128), jnp.float32)
        for k in range(8):
            root = lax.rsqrt(d[k][k])
            up = jnp.where(rows_of == k, y[k] * root, up)
            low = jnp.where(rows_of == k, v[k] * root, low)
        upper.append(jnp.where(cols_of >= rows_of + 8 * s, up, 0.0))
        inverse.append(low)
        if s < len(tasks):
            tasks[s]()
        if last:
            break
        x, w = [None] * 8, [None] * 8
        for k in reversed(range(8)):
            x[k] = y[k] * inv[k]
            w[k] = v[k] * inv[k]
            for j in reversed(range(k + 1, 8)):
                x[k] = x[k] - ratio[j][k] * x[j]
                w[k] = w[k] - ratio[j][k] * w[j]
        for g in range(s + 1, groups):
            f = near if g == s + 1 else [lane(left[g], 8 * s + k) for k in range(8)]
            for k in reversed(range(8)):
                if g > s + 1:
                    left[g] = left[g] - f[k] * x[k]
                right[g] = right[g] - f[k] * w[k]
    return jnp.concatenate(upper, axis=0), jnp.concatenate(inverse, axis=0)


def dot(a, b, dims=((1,), (0,))):
    return lax.dot_general(a, b, (dims, ((), ())), precision=HIGHEST, preferred_element_type=jnp.float32)

ROWS = ((1,), (1,))

def mul(a, b, dims=((1,), (0,))):
    return lax.dot_general(a, b, (dims, ((), ())), preferred_element_type=jnp.float32)


def split(x):
    pieces = []
    for _ in range(3):
        pieces.append(x.astype(jnp.bfloat16))
        x = x - pieces[-1].astype(jnp.float32)
    return pieces


def product(pieces, block):
    return sum(mul(pieces[p], block) for p in (2, 1, 0))


def solve(rows, pieces):
    return sum(mul(rows, pieces[p], ROWS) for p in (2, 1, 0))


def factor_rest(upper_1, inv_1, side, rest, lower_ref, pieces_ref, tasks=()):
    half = side.shape[0]
    pieces = split(inv_1)
    lower_21 = solve(side, pieces)
    rest = rest.astype(jnp.float32) - dot(lower_21, lower_21, ROWS)
    beside = dot(lower_21, inv_1)

    def store_left():
        lower_ref[half:, :half] = lower_21
        lower_ref[:half, half:] = jnp.zeros((half, half), jnp.float32)
        lower_ref[:half, :half] = upper_1.T

    def store_pieces():
        for p in range(3):
            pieces_ref[p, :half, :half] = pieces[p]
            pieces_ref[p, :half, half:] = jnp.zeros((half, half), jnp.bfloat16)

    upper_2, inv_2 = factor_tile(rest, [store_left, store_pieces] + list(tasks))
    inv_21 = -dot(inv_2, beside)
    lower_ref[half:, half:] = upper_2.T
    for p, (left, right) in enumerate(zip(split(inv_21), split(inv_2))):
        pieces_ref[p, half:, :half] = left
        pieces_ref[p, half:, half:] = right


def start_kernel(quarter_ref, upper_ref, inverse_ref):
    upper, inverse = factor_tile(quarter_ref[...].astype(jnp.float32))
    upper_ref[...] = upper
    inverse_ref[...] = inverse


def first_kernel(rest_ref, upper_ref, tile_inverse_ref, lower_ref, pieces_ref):
    half = rest_ref.shape[1]
    factor_rest(upper_ref[...], tile_inverse_ref[...], rest_ref[:half], rest_ref[half:], lower_ref, pieces_ref)


def second_start_kernel(
    top_10_ref, rest_10_ref, rest_01_ref, top_11_ref, rest_11_ref, pieces_0_ref,
    panel_ref, later_ref, upper_ref, inverse_ref,
):
    half = top_11_ref.shape[1]
    corner = rest_01_ref[:half].astype(jnp.float32).T.astype(jnp.bfloat16)
    left = jnp.concatenate([top_10_ref[...], rest_10_ref[:half]], axis=0)
    right = jnp.concatenate([corner, rest_10_ref[half:]], axis=0)
    panel = solve(jnp.concatenate([left, right], axis=1), pieces_0_ref).astype(jnp.bfloat16)
    above, below = panel[:half], panel[half:]
    top = (top_11_ref[...].astype(jnp.float32) - mul(above, above, ROWS)).astype(jnp.bfloat16)

    def side():
        panel_ref[...] = panel
        later_ref[:half] = (rest_11_ref[:half].astype(jnp.float32) - mul(below, above, ROWS)).astype(jnp.bfloat16)

    def rest():
        later_ref[half:] = (rest_11_ref[half:].astype(jnp.float32) - mul(below, below, ROWS)).astype(jnp.bfloat16)

    upper, inverse = factor_tile(top.astype(jnp.float32), (side, rest))
    upper_ref[...] = upper
    inverse_ref[...] = inverse


def second_kernel(
    ids_ref, rest_ref, upper_ref, tile_inverse_ref, pieces_0_ref, panel_ref, above_ref, other_ref,
    lower_ref, pieces_1_ref, mirror_ref, later_ref, above_0_ref, above_1_ref,
):
    half = rest_ref.shape[1]
    even = ids_ref[0] % 2 == 0
    tasks = []

    @pl.when(even)
    def _():
        above_0_ref[...] = above_ref[...]
        above_1_ref[...] = other_ref[...]

    @pl.when(jnp.logical_not(even))
    def _():
        above_0_ref[...] = other_ref[...]
        above_1_ref[...] = above_ref[...]

    for m in range(above_ref.shape[0]):
        def mirror(m=m):
            mirror_ref[m] = product(pieces_0_ref, above_0_ref[m]).astype(jnp.bfloat16)

        def later(m=m):
            change = mul(panel_ref[...], mirror_ref[m])
            later_ref[m] = (above_1_ref[m].astype(jnp.float32) - change).astype(jnp.bfloat16)

        tasks += [mirror, later]
    factor_rest(
        upper_ref[...], tile_inverse_ref[...], rest_ref[:half], rest_ref[half:], lower_ref, pieces_1_ref, tasks)


def update_kernel(
    ids_ref, column_0_ref, column_1_ref, blocks_ref, mirror_0_ref, later_ref,
    lower_0_ref, lower_1_ref, pieces_0_ref, pieces_1_ref, panel_10_ref,
    panels_ref, schur_ref, panels_here, schur_here, mirror_1_ref, panels_done, schur_done,
):
    row_blocks, col_blocks, width = blocks_ref.shape[:3]
    size = 2 if row_blocks % 2 == 0 else 1
    batches = range(0, row_blocks, size)
    ids = [i * ids_ref[2] + ids_ref[0] for i in range(row_blocks)]
    copies = []

    def send(source, target, semaphore):
        copies.append(pltpu.make_async_copy(source, target, semaphore))
        copies[-1].start()

    def below(solved, panel, lower_ref, start):
        parts = []
        for i in range(start, start + size):
            part = jnp.where(ids[i] > panel, solved[(i - start) * width:(i - start + 1) * width], 0.0)
            panels_here[i, panel] = jnp.where(ids[i] == panel, lower_ref[...], part)
            send(panels_here.at[i, panel], panels_ref.at[i, panel], panels_done.at[i, panel])
            parts.append(part)
        return jnp.concatenate(parts, axis=0).astype(jnp.bfloat16)

    def batch(column_ref, start):
        return column_ref[start:start + size].reshape(size * width, width)

    rounded_0 = [below(solve(batch(column_0_ref, b), pieces_0_ref), 0, lower_0_ref, b) for b in batches]
    columns = []
    for b, rounded in zip(batches, rounded_0):
        change = mul(rounded, panel_10_ref[...], ROWS)
        columns.append((batch(column_1_ref, b).astype(jnp.float32) - change).astype(jnp.bfloat16))
    for m in range(col_blocks):
        mirror_1_ref[m] = product(pieces_1_ref, later_ref[m]).astype(jnp.bfloat16)
    rounded_1 = [below(solve(column, pieces_1_ref), 1, lower_1_ref, b) for b, column in zip(batches, columns)]
    for b, left_0, left_1 in zip(batches, rounded_0, rounded_1):
        for m in range(col_blocks):
            change_0 = mul(left_0, mirror_0_ref[m])
            change_1 = mul(left_1, mirror_1_ref[m])
            for i in range(b, b + size):
                part = slice((i - b) * width, (i - b + 1) * width)
                block = blocks_ref[i, m].astype(jnp.float32) - change_0[part]
                block = block.astype(jnp.bfloat16).astype(jnp.float32) - change_1[part]
                keep = (ids[i] >= PANELS) & (m * ids_ref[3] + ids_ref[1] >= PANELS)
                schur_here[i, m] = jnp.where(keep, block, 0.0).astype(jnp.bfloat16)
        for i in range(b, b + size):
            send(schur_here.at[i], schur_ref.at[i], schur_done.at[i])
    for copy in copies:
        copy.wait()


FACTOR_COST = pl.CostEstimate(flops=10**6, bytes_accessed=10**4, transcendentals=0)


def call_factor(kernel, name, shapes, *operands, scratch=()):
    in_specs = [
        pl.BlockSpec(memory_space=pltpu.SMEM if x.dtype == jnp.int32 else pltpu.VMEM) for x in operands]
    return pl.pallas_call(
        kernel, in_specs=in_specs, out_shape=shapes, scratch_shapes=scratch, name=name, cost_estimate=FACTOR_COST,
        compiler_params=pltpu.CompilerParams(vmem_limit_bytes=VMEM_LIMIT),
    )(*operands)


def square(width, dtype=jnp.float32):
    return jax.ShapeDtypeStruct((width, width), dtype)


def update(ids, column_0, column_1, blocks, mirror_0, later, lower_0, lower_1, pieces_0, pieces_1, panel_10):
    row_blocks, col_blocks, width = blocks.shape[:3]
    panels = jax.ShapeDtypeStruct((row_blocks, PANELS, width, width), jnp.float32)
    schur = jax.ShapeDtypeStruct(blocks.shape, jnp.bfloat16)
    return pl.pallas_call(
        update_kernel,
        in_specs=[pl.BlockSpec(memory_space=pltpu.SMEM)] + [pl.BlockSpec(memory_space=pltpu.VMEM)] * 10,
        out_specs=[pl.BlockSpec(memory_space=pl.ANY)] * 2,
        out_shape=[panels, schur],
        scratch_shapes=[
            pltpu.VMEM(panels.shape, panels.dtype),
            pltpu.VMEM(schur.shape, schur.dtype),
            pltpu.VMEM((col_blocks, width, width), jnp.bfloat16),
            pltpu.SemaphoreType.DMA((row_blocks, PANELS)),
            pltpu.SemaphoreType.DMA((row_blocks,)),
        ],
        compiler_params=pltpu.CompilerParams(vmem_limit_bytes=VMEM_LIMIT),
        cost_estimate=pl.CostEstimate(flops=2 * 10**9, bytes_accessed=6 * 10**6, transcendentals=0),
        name="solve_and_update",
    )(ids, column_0, column_1, blocks, mirror_0, later, lower_0, lower_1, pieces_0, pieces_1, panel_10)


def pack_kernel(kernel_ref, quarters_ref, semaphores):
    half = quarters_ref.shape[1]
    copies = []
    for q, (row, col) in enumerate(((0, 0), (1, 0), (1, 1))):
        source = kernel_ref.at[0, 0, 0, 0, pl.ds(row * half, half), pl.ds(col * half, half)]
        copies.append(pltpu.make_async_copy(source, quarters_ref.at[pl.ds(q * half, half)], semaphores.at[q]))
    for copy in copies:
        copy.start()
    for copy in copies:
        copy.wait()


def pack(kernel):
    half = kernel.shape[-1] // 2
    return pl.pallas_call(
        pack_kernel,
        in_specs=[pl.BlockSpec(memory_space=pltpu.HBM)],
        out_shape=jax.ShapeDtypeStruct((3 * half, half), kernel.dtype),
        scratch_shapes=[pltpu.SemaphoreType.DMA((3,))],
        compiler_params=pltpu.CompilerParams(vmem_limit_bytes=2 * 1024 * 1024),
        name="pack",
    )(kernel)


def swap(block, axis, distance):
    count = lax.axis_size(axis)
    return lax.ppermute(block, axis, [(d, d ^ distance) for d in range(count)])


HOLDERS = ((0, 0), (0, 1), (1, 0), (1, 1))


def diagonal_along(quarters, my_col):
    col_count = lax.axis_size("col")
    along = quarters
    for chip in range(1, col_count // 2):
        pairs = [(r * col_count + core, r * col_count + chip * 2 + core) for r, core in HOLDERS]
        got = lax.ppermute(quarters, ("row", "col"), pairs)
        along = jnp.where(my_col // 2 == chip, got, along)
    return along


def diagonal_down(along, my_row):
    first, second = along, along
    for step in range(1, lax.axis_size("row")):
        got = swap(along, "row", step)
        first = jnp.where(my_row == step, got, first)
        second = jnp.where(my_row == step ^ 1, got, second)
    return jnp.stack([first, second])


def both_cores(pair, my_col):
    other = swap(pair, "col", 1)
    even = my_col % 2 == 0
    left = jnp.where(even, pair, other)
    right = jnp.where(even, other, pair)
    return left[0], right[0], left[1], right[1]


def first_reach(block):
    return block, swap(block, "row", 2)


def other_reaches(block, got, my_row):
    reach = 2
    while True:
        block = jnp.where((my_row >= reach) & (my_row < 2 * reach), got, block)
        reach *= 2
        if reach >= lax.axis_size("row"):
            return block
        got = swap(block, "row", reach)


def first_stride(block):
    chips = lax.axis_size("col") // 2
    pairs = [(core, core + chips) for core in range(2)]
    return block, lax.ppermute(block, "col", pairs)


def other_strides(block, got, my_col):
    chips = lax.axis_size("col") // 2
    stride = chips // 2
    while True:
        block = jnp.where((my_col // 2) % (2 * stride) == stride, got, block)
        stride //= 2
        if stride == 0:
            return block
        if stride == 1:
            got = swap(block, "col", 2)
        else:
            sources = [chip * 2 + core for chip in range(0, chips, 2 * stride) for core in range(2)]
            got = lax.ppermute(block, "col", [(s, s + 2 * stride) for s in sources])


def per_device(kernel):
    my_row = lax.axis_index("row")
    my_col = lax.axis_index("col")
    even = my_col % 2 == 0
    blocks = kernel[0, :, 0]
    col_blocks, width = blocks.shape[1:3]
    half = width // 2
    ids = jnp.stack([my_row, my_col, lax.axis_size("row"), lax.axis_size("col")]).astype(jnp.int32)
    quarters = pack(kernel)
    rows, _ = lax.optimization_barrier((blocks[:, 0], quarters))
    rows, rows_got = first_stride(rows)
    along = diagonal_along(quarters, my_col)
    pair = diagonal_down(along, my_row)
    pair, above = lax.optimization_barrier((pair, blocks[0]))
    above, above_got = first_reach(above)
    pair, rows, rows_got = lax.optimization_barrier((pair, rows, rows_got))
    block_00, block_01, block_10, block_11 = both_cores(pair, my_col)
    rows = other_strides(rows, rows_got, my_col)
    upper_0, tile_inverse_0 = call_factor(start_kernel, "factor_start", [square(half)] * 2, block_00[:half])
    above, above_got, tile_inverse_0 = lax.optimization_barrier((above, above_got, tile_inverse_0))
    above = other_reaches(above, above_got, my_row)
    above_other = swap(above, "row", 1)
    pieces = jax.ShapeDtypeStruct((3, width, width), jnp.bfloat16)
    lower_0, pieces_0 = call_factor(
        first_kernel, "factor_first", [square(width), pieces], block_00[half:], upper_0, tile_inverse_0)
    panel_10, rest_11, upper_1, tile_inverse_1 = call_factor(
        second_start_kernel, "factor_second_start",
        [square(width, jnp.bfloat16), jax.ShapeDtypeStruct((width, half), jnp.bfloat16), square(half), square(half)],
        block_10[:half], block_10[half:], block_01[half:], block_11[:half], block_11[half:], pieces_0)
    rows, above, above_other, tile_inverse_1 = lax.optimization_barrier((rows, above, above_other, tile_inverse_1))
    other = swap(rows, "col", 1)
    mirror = jax.ShapeDtypeStruct((col_blocks, width, width), jnp.bfloat16)
    lower_1, pieces_1, mirror_0, later = call_factor(
        second_kernel, "factor_second", [square(width), pieces, mirror, mirror],
        ids, rest_11, upper_1, tile_inverse_1, pieces_0, panel_10, above, above_other,
        scratch=[pltpu.VMEM(mirror.shape, mirror.dtype)] * 2)
    other, lower_1 = lax.optimization_barrier((other, lower_1))
    column_0 = jnp.where(even, rows, other)
    column_1 = jnp.where(even, other, rows)
    panels, schur = update(
        ids, column_0, column_1, blocks, mirror_0, later, lower_0, lower_1, pieces_0, pieces_1, panel_10)
    return (panels[None], schur[None, :, None])


def solution(mesh):
    in_specs = (P("row", None, "col", None, None, None),)
    out_specs = (P("row", None, None, None, None), P("row", None, "col", None, None, None))
    return jax.shard_map(
        per_device, mesh=mesh, in_specs=in_specs, out_specs=out_specs, check_vma=False
    )
```

```python
import jax
import jax.numpy as jnp
from jax import lax
from jax.experimental import pallas as pl
from jax.experimental.pallas import tpu as pltpu
from jax.sharding import PartitionSpec as P

PANELS = 2
HIGHEST = lax.Precision.HIGHEST
VMEM_LIMIT = 20 * 1024 * 1024

def spread(row):
    return jnp.broadcast_to(row, (8, row.shape[1]))


def lane(tile, k):
    return jnp.broadcast_to(tile[:, k:k + 1], (8, 128))


def factor_tile(matrix, tasks=()):
    groups = 16
    rows_of = lax.broadcasted_iota(jnp.int32, (8, 128), 0)
    cols_of = lax.broadcasted_iota(jnp.int32, (8, 128), 1)
    left = [matrix[8 * g:8 * g + 8, :] for g in range(groups)]
    right = [(cols_of == rows_of + 8 * g).astype(jnp.float32) for g in range(groups)]
    upper, inverse = [], []
    for s in range(groups):
        y = [spread(left[s][k:k + 1, :]) for k in range(8)]
        v = [spread(right[s][k:k + 1, :]) for k in range(8)]
        d = [[lane(y[i], 8 * s + k) if k >= i else None for k in range(8)] for i in range(8)]
        last = s + 1 == groups
        near = None if last else [lane(left[s + 1], 8 * s + k) for k in range(8)]
        e = None if last else list(near)
        ratio = [[None] * 8 for _ in range(8)]
        inv = []
        for k in range(8):
            inv.append(pl.reciprocal(d[k][k], approx=True))
            for i in range(k + 1, 8):
                ratio[i][k] = d[k][i] * inv[k]
                for j in range(i, 8):
                    d[i][j] = d[i][j] - ratio[i][k] * d[k][j]
                y[i] = y[i] - ratio[i][k] * y[k]
                v[i] = v[i] - ratio[i][k] * v[k]
            if not last:
                left[s + 1] = left[s + 1] - e[k] * inv[k] * y[k]
                for j in range(k + 1, 8):
                    e[j] = e[j] - e[k] * ratio[j][k]
        up = jnp.zeros((8, 128), jnp.float32)
        low = jnp.zeros((8, 128), jnp.float32)
        for k in range(8):
            root = lax.rsqrt(d[k][k])
            up = jnp.where(rows_of == k, y[k] * root, up)
            low = jnp.where(rows_of == k, v[k] * root, low)
        upper.append(jnp.where(cols_of >= rows_of + 8 * s, up, 0.0))
        inverse.append(low)
        if s < len(tasks):
            tasks[s]()
        if last:
            break
        x, w = [None] * 8, [None] * 8
        for k in reversed(range(8)):
            x[k] = y[k] * inv[k]
            w[k] = v[k] * inv[k]
            for j in reversed(range(k + 1, 8)):
                x[k] = x[k] - ratio[j][k] * x[j]
                w[k] = w[k] - ratio[j][k] * w[j]
        for g in range(s + 1, groups):
            f = near if g == s + 1 else [lane(left[g], 8 * s + k) for k in range(8)]
            for k in reversed(range(8)):
                if g > s + 1:
                    left[g] = left[g] - f[k] * x[k]
                right[g] = right[g] - f[k] * w[k]
    return jnp.concatenate(upper, axis=0), jnp.concatenate(inverse, axis=0)


def dot(a, b, dims=((1,), (0,))):
    return lax.dot_general(a, b, (dims, ((), ())), precision=HIGHEST, preferred_element_type=jnp.float32)

ROWS = ((1,), (1,))

def mul(a, b, dims=((1,), (0,))):
    return lax.dot_general(a, b, (dims, ((), ())), preferred_element_type=jnp.float32)


def split(x):
    pieces = []
    for _ in range(3):
        pieces.append(x.astype(jnp.bfloat16))
        x = x - pieces[-1].astype(jnp.float32)
    return pieces


def product(pieces, block):
    return sum(mul(pieces[p], block) for p in (2, 1, 0))


def solve(rows, pieces):
    return sum(mul(rows, pieces[p], ROWS) for p in (2, 1, 0))


def factor_rest(upper_1, inv_1, side, rest, lower_ref, pieces_ref, tasks=()):
    half = side.shape[0]
    pieces = split(inv_1)
    lower_21 = solve(side, pieces)
    rest = rest.astype(jnp.float32) - dot(lower_21, lower_21, ROWS)
    beside = dot(lower_21, inv_1)

    def store_left():
        lower_ref[half:, :half] = lower_21
        lower_ref[:half, half:] = jnp.zeros((half, half), jnp.float32)
        lower_ref[:half, :half] = upper_1.T

    def store_pieces():
        for p in range(3):
            pieces_ref[p, :half, :half] = pieces[p]
            pieces_ref[p, :half, half:] = jnp.zeros((half, half), jnp.bfloat16)

    upper_2, inv_2 = factor_tile(rest, [store_left, store_pieces] + list(tasks))
    inv_21 = -dot(inv_2, beside)
    lower_ref[half:, half:] = upper_2.T
    for p, (left, right) in enumerate(zip(split(inv_21), split(inv_2))):
        pieces_ref[p, half:, :half] = left
        pieces_ref[p, half:, half:] = right


def start_kernel(quarter_ref, upper_ref, inverse_ref):
    upper, inverse = factor_tile(quarter_ref[...].astype(jnp.float32))
    upper_ref[...] = upper
    inverse_ref[...] = inverse


def first_kernel(rest_ref, upper_ref, tile_inverse_ref, lower_ref, pieces_ref):
    half = rest_ref.shape[1]
    factor_rest(upper_ref[...], tile_inverse_ref[...], rest_ref[:half], rest_ref[half:], lower_ref, pieces_ref)


def second_start_kernel(
    top_10_ref, rest_10_ref, rest_01_ref, top_11_ref, rest_11_ref, pieces_0_ref,
    panel_ref, later_ref, upper_ref, inverse_ref,
):
    half = top_11_ref.shape[1]
    corner = rest_01_ref[:half].astype(jnp.float32).T.astype(jnp.bfloat16)
    left = jnp.concatenate([top_10_ref[...], rest_10_ref[:half]], axis=0)
    right = jnp.concatenate([corner, rest_10_ref[half:]], axis=0)
    panel = solve(jnp.concatenate([left, right], axis=1), pieces_0_ref).astype(jnp.bfloat16)
    above, below = panel[:half], panel[half:]
    top = (top_11_ref[...].astype(jnp.float32) - mul(above, above, ROWS)).astype(jnp.bfloat16)

    def side():
        panel_ref[...] = panel
        later_ref[:half] = (rest_11_ref[:half].astype(jnp.float32) - mul(below, above, ROWS)).astype(jnp.bfloat16)

    def rest():
        later_ref[half:] = (rest_11_ref[half:].astype(jnp.float32) - mul(below, below, ROWS)).astype(jnp.bfloat16)

    upper, inverse = factor_tile(top.astype(jnp.float32), (side, rest))
    upper_ref[...] = upper
    inverse_ref[...] = inverse


def second_kernel(
    ids_ref, rest_ref, upper_ref, tile_inverse_ref, pieces_0_ref, panel_ref, above_ref, other_ref,
    lower_ref, pieces_1_ref, mirror_ref, later_ref, above_0_ref, above_1_ref,
):
    half = rest_ref.shape[1]
    even = ids_ref[0] % 2 == 0
    tasks = []

    @pl.when(even)
    def _():
        above_0_ref[...] = above_ref[...]
        above_1_ref[...] = other_ref[...]

    @pl.when(jnp.logical_not(even))
    def _():
        above_0_ref[...] = other_ref[...]
        above_1_ref[...] = above_ref[...]

    parts = (pl.ds(0, half), pl.ds(half, half))
    for m in range(above_ref.shape[0]):
        for part in parts:
            def mirror(m=m, part=part):
                terms = [mul(pieces_0_ref[p, part], above_0_ref[m]) for p in (2, 1, 0)]
                mirror_ref[m, part] = sum(terms).astype(jnp.bfloat16)
            tasks.append(mirror)
    for m in range(above_ref.shape[0]):
        for part in parts:
            def later(m=m, part=part):
                change = mul(panel_ref[part], mirror_ref[m])
                later_ref[m, part] = (above_1_ref[m, part].astype(jnp.float32) - change).astype(jnp.bfloat16)
            tasks.append(later)
    factor_rest(
        upper_ref[...], tile_inverse_ref[...], rest_ref[:half], rest_ref[half:], lower_ref, pieces_1_ref, tasks)


def update_kernel(
    ids_ref, column_0_ref, column_1_ref, blocks_ref, mirror_0_ref, later_ref,
    lower_0_ref, lower_1_ref, pieces_0_ref, pieces_1_ref, panel_10_ref,
    panels_ref, schur_ref, panels_here, schur_here, mirror_1_ref, panels_done, schur_done,
):
    row_blocks, col_blocks, width = blocks_ref.shape[:3]
    size = 2 if row_blocks % 2 == 0 else 1
    batches = range(0, row_blocks, size)
    ids = [i * ids_ref[2] + ids_ref[0] for i in range(row_blocks)]
    copies = []

    def send(source, target, semaphore):
        copies.append(pltpu.make_async_copy(source, target, semaphore))
        copies[-1].start()

    def below(solved, panel, lower_ref, start):
        parts = []
        for i in range(start, start + size):
            part = jnp.where(ids[i] > panel, solved[(i - start) * width:(i - start + 1) * width], 0.0)
            panels_here[i, panel] = jnp.where(ids[i] == panel, lower_ref[...], part)
            send(panels_here.at[i, panel], panels_ref.at[i, panel], panels_done.at[i, panel])
            parts.append(part)
        return jnp.concatenate(parts, axis=0).astype(jnp.bfloat16)

    def batch(column_ref, start):
        return column_ref[start:start + size].reshape(size * width, width)

    rounded_0 = [below(solve(batch(column_0_ref, b), pieces_0_ref), 0, lower_0_ref, b) for b in batches]
    columns = []
    for b, rounded in zip(batches, rounded_0):
        change = mul(rounded, panel_10_ref[...], ROWS)
        columns.append((batch(column_1_ref, b).astype(jnp.float32) - change).astype(jnp.bfloat16))
    for m in range(col_blocks):
        mirror_1_ref[m] = product(pieces_1_ref, later_ref[m]).astype(jnp.bfloat16)
    rounded_1 = [below(solve(column, pieces_1_ref), 1, lower_1_ref, b) for b, column in zip(batches, columns)]
    for b, left_0, left_1 in zip(batches, rounded_0, rounded_1):
        for m in range(col_blocks):
            change_0 = mul(left_0, mirror_0_ref[m])
            change_1 = mul(left_1, mirror_1_ref[m])
            for i in range(b, b + size):
                part = slice((i - b) * width, (i - b + 1) * width)
                block = blocks_ref[i, m].astype(jnp.float32) - change_0[part]
                block = block.astype(jnp.bfloat16).astype(jnp.float32) - change_1[part]
                keep = (ids[i] >= PANELS) & (m * ids_ref[3] + ids_ref[1] >= PANELS)
                schur_here[i, m] = jnp.where(keep, block, 0.0).astype(jnp.bfloat16)
        for i in range(b, b + size):
            send(schur_here.at[i], schur_ref.at[i], schur_done.at[i])
    for copy in copies:
        copy.wait()


FACTOR_COST = pl.CostEstimate(flops=10**6, bytes_accessed=10**4, transcendentals=0)


def call_factor(kernel, name, shapes, *operands, scratch=()):
    in_specs = [
        pl.BlockSpec(memory_space=pltpu.SMEM if x.dtype == jnp.int32 else pltpu.VMEM) for x in operands]
    return pl.pallas_call(
        kernel, in_specs=in_specs, out_shape=shapes, scratch_shapes=scratch, name=name, cost_estimate=FACTOR_COST,
        compiler_params=pltpu.CompilerParams(vmem_limit_bytes=VMEM_LIMIT),
    )(*operands)


def square(width, dtype=jnp.float32):
    return jax.ShapeDtypeStruct((width, width), dtype)


def update(ids, column_0, column_1, blocks, mirror_0, later, lower_0, lower_1, pieces_0, pieces_1, panel_10):
    row_blocks, col_blocks, width = blocks.shape[:3]
    panels = jax.ShapeDtypeStruct((row_blocks, PANELS, width, width), jnp.float32)
    schur = jax.ShapeDtypeStruct(blocks.shape, jnp.bfloat16)
    return pl.pallas_call(
        update_kernel,
        in_specs=[pl.BlockSpec(memory_space=pltpu.SMEM)] + [pl.BlockSpec(memory_space=pltpu.VMEM)] * 10,
        out_specs=[pl.BlockSpec(memory_space=pl.ANY)] * 2,
        out_shape=[panels, schur],
        scratch_shapes=[
            pltpu.VMEM(panels.shape, panels.dtype),
            pltpu.VMEM(schur.shape, schur.dtype),
            pltpu.VMEM((col_blocks, width, width), jnp.bfloat16),
            pltpu.SemaphoreType.DMA((row_blocks, PANELS)),
            pltpu.SemaphoreType.DMA((row_blocks,)),
        ],
        compiler_params=pltpu.CompilerParams(vmem_limit_bytes=VMEM_LIMIT),
        cost_estimate=pl.CostEstimate(flops=2 * 10**9, bytes_accessed=6 * 10**6, transcendentals=0),
        name="solve_and_update",
    )(ids, column_0, column_1, blocks, mirror_0, later, lower_0, lower_1, pieces_0, pieces_1, panel_10)


def pack_kernel(kernel_ref, quarters_ref, semaphores):
    half = quarters_ref.shape[1]
    copies = []
    for q, (row, col) in enumerate(((0, 0), (1, 0), (1, 1))):
        source = kernel_ref.at[0, 0, 0, 0, pl.ds(row * half, half), pl.ds(col * half, half)]
        copies.append(pltpu.make_async_copy(source, quarters_ref.at[pl.ds(q * half, half)], semaphores.at[q]))
    for copy in copies:
        copy.start()
    for copy in copies:
        copy.wait()


def pack(kernel):
    half = kernel.shape[-1] // 2
    return pl.pallas_call(
        pack_kernel,
        in_specs=[pl.BlockSpec(memory_space=pltpu.HBM)],
        out_shape=jax.ShapeDtypeStruct((3 * half, half), kernel.dtype),
        scratch_shapes=[pltpu.SemaphoreType.DMA((3,))],
        compiler_params=pltpu.CompilerParams(vmem_limit_bytes=2 * 1024 * 1024),
        name="pack",
    )(kernel)


def swap(block, axis, distance):
    count = lax.axis_size(axis)
    return lax.ppermute(block, axis, [(d, d ^ distance) for d in range(count)])


HOLDERS = ((0, 0), (0, 1), (1, 0), (1, 1))


def diagonal_along(quarters, my_col):
    col_count = lax.axis_size("col")
    along = quarters
    for chip in range(1, col_count // 2):
        pairs = [(r * col_count + core, r * col_count + chip * 2 + core) for r, core in HOLDERS]
        got = lax.ppermute(quarters, ("row", "col"), pairs)
        along = jnp.where(my_col // 2 == chip, got, along)
    return along


def diagonal_down(along, my_row):
    first, second = along, along
    for step in range(1, lax.axis_size("row")):
        got = swap(along, "row", step)
        first = jnp.where(my_row == step, got, first)
        second = jnp.where(my_row == step ^ 1, got, second)
    return jnp.stack([first, second])


def both_cores(pair, my_col):
    other = swap(pair, "col", 1)
    even = my_col % 2 == 0
    left = jnp.where(even, pair, other)
    right = jnp.where(even, other, pair)
    return left[0], right[0], left[1], right[1]


def first_reach(block):
    return block, swap(block, "row", 2)


def other_reaches(block, got, my_row):
    reach = 2
    while True:
        block = jnp.where((my_row >= reach) & (my_row < 2 * reach), got, block)
        reach *= 2
        if reach >= lax.axis_size("row"):
            return block
        got = swap(block, "row", reach)


def first_stride(block):
    chips = lax.axis_size("col") // 2
    pairs = [(core, core + chips) for core in range(2)]
    return block, lax.ppermute(block, "col", pairs)


def other_strides(block, got, my_col):
    chips = lax.axis_size("col") // 2
    stride = chips // 2
    while True:
        block = jnp.where((my_col // 2) % (2 * stride) == stride, got, block)
        stride //= 2
        if stride == 0:
            return block
        if stride == 1:
            got = swap(block, "col", 2)
        else:
            sources = [chip * 2 + core for chip in range(0, chips, 2 * stride) for core in range(2)]
            got = lax.ppermute(block, "col", [(s, s + 2 * stride) for s in sources])


def per_device(kernel):
    my_row = lax.axis_index("row")
    my_col = lax.axis_index("col")
    even = my_col % 2 == 0
    blocks = kernel[0, :, 0]
    col_blocks, width = blocks.shape[1:3]
    half = width // 2
    ids = jnp.stack([my_row, my_col, lax.axis_size("row"), lax.axis_size("col")]).astype(jnp.int32)
    quarters = pack(kernel)
    rows, above, _ = lax.optimization_barrier((blocks[:, 0], blocks[0], quarters))
    rows, rows_got = first_stride(rows)
    above, above_got = first_reach(above)
    along = diagonal_along(quarters, my_col)
    pair = diagonal_down(along, my_row)
    pair, rows, rows_got = lax.optimization_barrier((pair, rows, rows_got))
    block_00, block_01, block_10, block_11 = both_cores(pair, my_col)
    rows = other_strides(rows, rows_got, my_col)
    upper_0, tile_inverse_0 = call_factor(start_kernel, "factor_start", [square(half)] * 2, block_00[:half])
    above, above_got, tile_inverse_0 = lax.optimization_barrier((above, above_got, tile_inverse_0))
    above = other_reaches(above, above_got, my_row)
    above_other = swap(above, "row", 1)
    pieces = jax.ShapeDtypeStruct((3, width, width), jnp.bfloat16)
    lower_0, pieces_0 = call_factor(
        first_kernel, "factor_first", [square(width), pieces], block_00[half:], upper_0, tile_inverse_0)
    panel_10, rest_11, upper_1, tile_inverse_1 = call_factor(
        second_start_kernel, "factor_second_start",
        [square(width, jnp.bfloat16), jax.ShapeDtypeStruct((width, half), jnp.bfloat16), square(half), square(half)],
        block_10[:half], block_10[half:], block_01[half:], block_11[:half], block_11[half:], pieces_0)
    rows, above, above_other, tile_inverse_1 = lax.optimization_barrier((rows, above, above_other, tile_inverse_1))
    other = swap(rows, "col", 1)
    mirror = jax.ShapeDtypeStruct((col_blocks, width, width), jnp.bfloat16)
    lower_1, pieces_1, mirror_0, later = call_factor(
        second_kernel, "factor_second", [square(width), pieces, mirror, mirror],
        ids, rest_11, upper_1, tile_inverse_1, pieces_0, panel_10, above, above_other,
        scratch=[pltpu.VMEM(mirror.shape, mirror.dtype)] * 2)
    other, lower_1 = lax.optimization_barrier((other, lower_1))
    column_0 = jnp.where(even, rows, other)
    column_1 = jnp.where(even, other, rows)
    panels, schur = update(
        ids, column_0, column_1, blocks, mirror_0, later, lower_0, lower_1, pieces_0, pieces_1, panel_10)
    return (panels[None], schur[None, :, None])


def solution(mesh):
    in_specs = (P("row", None, "col", None, None, None),)
    out_specs = (P("row", None, None, None, None), P("row", None, "col", None, None, None))
    return jax.shard_map(
        per_device, mesh=mesh, in_specs=in_specs, out_specs=out_specs, check_vma=False
    )
```

```python
import jax
import jax.numpy as jnp
from jax import lax
from jax.experimental import pallas as pl
from jax.experimental.pallas import tpu as pltpu
from jax.sharding import PartitionSpec as P

PANELS = 2
HIGHEST = lax.Precision.HIGHEST
VMEM_LIMIT = 20 * 1024 * 1024

def spread(row):
    return jnp.broadcast_to(row, (8, row.shape[1]))


def lane(tile, k):
    return jnp.broadcast_to(tile[:, k:k + 1], (8, 128))


def factor_tile(matrix, tasks=()):
    groups = 16
    rows_of = lax.broadcasted_iota(jnp.int32, (8, 128), 0)
    cols_of = lax.broadcasted_iota(jnp.int32, (8, 128), 1)
    left = [matrix[8 * g:8 * g + 8, :] for g in range(groups)]
    right = [(cols_of == rows_of + 8 * g).astype(jnp.float32) for g in range(groups)]
    upper, inverse = [], []
    for s in range(groups):
        y = [spread(left[s][k:k + 1, :]) for k in range(8)]
        v = [spread(right[s][k:k + 1, :]) for k in range(8)]
        d = [[lane(y[i], 8 * s + k) if k >= i else None for k in range(8)] for i in range(8)]
        last = s + 1 == groups
        columns = [[lane(left[g], 8 * s + k) for k in range(8)] for g in range(s + 1, groups)]
        e = list(columns[0]) if not last else None
        ratio = [[None] * 8 for _ in range(8)]
        inv = []
        for k in range(8):
            inv.append(pl.reciprocal(d[k][k], approx=True))
            for i in range(k + 1, 8):
                ratio[i][k] = d[k][i] * inv[k]
                for j in range(i, 8):
                    d[i][j] = d[i][j] - ratio[i][k] * d[k][j]
                y[i] = y[i] - ratio[i][k] * y[k]
                v[i] = v[i] - ratio[i][k] * v[k]
            if not last:
                left[s + 1] = left[s + 1] - e[k] * inv[k] * y[k]
                for j in range(k + 1, 8):
                    e[j] = e[j] - e[k] * ratio[j][k]
        up = jnp.zeros((8, 128), jnp.float32)
        low = jnp.zeros((8, 128), jnp.float32)
        for k in range(8):
            root = lax.rsqrt(d[k][k])
            up = jnp.where(rows_of == k, y[k] * root, up)
            low = jnp.where(rows_of == k, v[k] * root, low)
        upper.append(jnp.where(cols_of >= rows_of + 8 * s, up, 0.0))
        inverse.append(low)
        if s < len(tasks):
            tasks[s]()
        if last:
            break
        x, w = [None] * 8, [None] * 8
        for k in reversed(range(8)):
            x[k] = y[k] * inv[k]
            w[k] = v[k] * inv[k]
            for j in reversed(range(k + 1, 8)):
                x[k] = x[k] - ratio[j][k] * x[j]
                w[k] = w[k] - ratio[j][k] * w[j]
        for g in range(s + 1, groups):
            f = columns[g - s - 1]
            for k in reversed(range(8)):
                if g > s + 1:
                    left[g] = left[g] - f[k] * x[k]
                right[g] = right[g] - f[k] * w[k]
    return jnp.concatenate(upper, axis=0), jnp.concatenate(inverse, axis=0)


def dot(a, b, dims=((1,), (0,))):
    return lax.dot_general(a, b, (dims, ((), ())), precision=HIGHEST, preferred_element_type=jnp.float32)

ROWS = ((1,), (1,))

def mul(a, b, dims=((1,), (0,))):
    return lax.dot_general(a, b, (dims, ((), ())), preferred_element_type=jnp.float32)


def split(x):
    pieces = []
    for _ in range(3):
        pieces.append(x.astype(jnp.bfloat16))
        x = x - pieces[-1].astype(jnp.float32)
    return pieces


def product(pieces, block):
    return sum(mul(pieces[p], block) for p in (2, 1, 0))


def solve(rows, pieces):
    return sum(mul(rows, pieces[p], ROWS) for p in (2, 1, 0))


def factor_rest(upper_1, inv_1, side, rest, lower_ref, pieces_ref, tasks=()):
    half = side.shape[0]
    pieces = split(inv_1)
    lower_21 = solve(side, pieces)
    rest = rest.astype(jnp.float32) - dot(lower_21, lower_21, ROWS)
    beside = dot(lower_21, inv_1)

    def store_left():
        lower_ref[half:, :half] = lower_21
        lower_ref[:half, half:] = jnp.zeros((half, half), jnp.float32)
        lower_ref[:half, :half] = upper_1.T

    def store_pieces():
        for p in range(3):
            pieces_ref[p, :half, :half] = pieces[p]
            pieces_ref[p, :half, half:] = jnp.zeros((half, half), jnp.bfloat16)

    upper_2, inv_2 = factor_tile(rest, [store_left, store_pieces] + list(tasks))
    inv_21 = -dot(inv_2, beside)
    lower_ref[half:, half:] = upper_2.T
    for p, (left, right) in enumerate(zip(split(inv_21), split(inv_2))):
        pieces_ref[p, half:, :half] = left
        pieces_ref[p, half:, half:] = right


def start_kernel(quarter_ref, upper_ref, inverse_ref):
    upper, inverse = factor_tile(quarter_ref[...].astype(jnp.float32))
    upper_ref[...] = upper
    inverse_ref[...] = inverse


def first_kernel(rest_ref, upper_ref, tile_inverse_ref, lower_ref, pieces_ref):
    half = rest_ref.shape[1]
    factor_rest(upper_ref[...], tile_inverse_ref[...], rest_ref[:half], rest_ref[half:], lower_ref, pieces_ref)


def second_start_kernel(
    top_10_ref, rest_10_ref, rest_01_ref, top_11_ref, rest_11_ref, pieces_0_ref,
    panel_ref, later_ref, upper_ref, inverse_ref,
):
    half = top_11_ref.shape[1]
    corner = rest_01_ref[:half].astype(jnp.float32).T.astype(jnp.bfloat16)
    left = jnp.concatenate([top_10_ref[...], rest_10_ref[:half]], axis=0)
    right = jnp.concatenate([corner, rest_10_ref[half:]], axis=0)
    panel = solve(jnp.concatenate([left, right], axis=1), pieces_0_ref).astype(jnp.bfloat16)
    above, below = panel[:half], panel[half:]
    top = (top_11_ref[...].astype(jnp.float32) - mul(above, above, ROWS)).astype(jnp.bfloat16)

    def side():
        panel_ref[...] = panel
        later_ref[:half] = (rest_11_ref[:half].astype(jnp.float32) - mul(below, above, ROWS)).astype(jnp.bfloat16)

    def rest():
        later_ref[half:] = (rest_11_ref[half:].astype(jnp.float32) - mul(below, below, ROWS)).astype(jnp.bfloat16)

    upper, inverse = factor_tile(top.astype(jnp.float32), (side, rest))
    upper_ref[...] = upper
    inverse_ref[...] = inverse


def second_kernel(
    ids_ref, rest_ref, upper_ref, tile_inverse_ref, pieces_0_ref, panel_ref, above_ref, other_ref,
    lower_ref, pieces_1_ref, mirror_ref, later_ref, above_0_ref, above_1_ref,
):
    half = rest_ref.shape[1]
    even = ids_ref[0] % 2 == 0
    tasks = []

    @pl.when(even)
    def _():
        above_0_ref[...] = above_ref[...]
        above_1_ref[...] = other_ref[...]

    @pl.when(jnp.logical_not(even))
    def _():
        above_0_ref[...] = other_ref[...]
        above_1_ref[...] = above_ref[...]

    parts = (pl.ds(0, half), pl.ds(half, half))
    for m in range(above_ref.shape[0]):
        for part in parts:
            def mirror(m=m, part=part):
                terms = [mul(pieces_0_ref[p, part], above_0_ref[m]) for p in (2, 1, 0)]
                mirror_ref[m, part] = sum(terms).astype(jnp.bfloat16)
            tasks.append(mirror)
    for m in range(above_ref.shape[0]):
        for part in parts:
            def later(m=m, part=part):
                change = mul(panel_ref[part], mirror_ref[m])
                later_ref[m, part] = (above_1_ref[m, part].astype(jnp.float32) - change).astype(jnp.bfloat16)
            tasks.append(later)
    factor_rest(
        upper_ref[...], tile_inverse_ref[...], rest_ref[:half], rest_ref[half:], lower_ref, pieces_1_ref, tasks)


def update_kernel(
    ids_ref, column_0_ref, column_1_ref, blocks_ref, mirror_0_ref, later_ref,
    lower_0_ref, lower_1_ref, pieces_0_ref, pieces_1_ref, panel_10_ref,
    panels_ref, schur_ref, panels_here, schur_here, mirror_1_ref, panels_done, schur_done,
):
    row_blocks, col_blocks, width = blocks_ref.shape[:3]
    size = 2 if row_blocks % 2 == 0 else 1
    batches = range(0, row_blocks, size)
    ids = [i * ids_ref[2] + ids_ref[0] for i in range(row_blocks)]
    copies = []

    def send(source, target, semaphore):
        copies.append(pltpu.make_async_copy(source, target, semaphore))
        copies[-1].start()

    def below(solved, panel, lower_ref, start):
        parts = []
        for i in range(start, start + size):
            part = jnp.where(ids[i] > panel, solved[(i - start) * width:(i - start + 1) * width], 0.0)
            panels_here[i, panel] = jnp.where(ids[i] == panel, lower_ref[...], part)
            send(panels_here.at[i, panel], panels_ref.at[i, panel], panels_done.at[i, panel])
            parts.append(part)
        return jnp.concatenate(parts, axis=0).astype(jnp.bfloat16)

    def batch(column_ref, start):
        return column_ref[start:start + size].reshape(size * width, width)

    rounded_0 = [below(solve(batch(column_0_ref, b), pieces_0_ref), 0, lower_0_ref, b) for b in batches]
    columns = []
    for b, rounded in zip(batches, rounded_0):
        change = mul(rounded, panel_10_ref[...], ROWS)
        columns.append((batch(column_1_ref, b).astype(jnp.float32) - change).astype(jnp.bfloat16))
    for m in range(col_blocks):
        mirror_1_ref[m] = product(pieces_1_ref, later_ref[m]).astype(jnp.bfloat16)
    rounded_1 = [below(solve(column, pieces_1_ref), 1, lower_1_ref, b) for b, column in zip(batches, columns)]
    for b, left_0, left_1 in zip(batches, rounded_0, rounded_1):
        for m in range(col_blocks):
            change_0 = mul(left_0, mirror_0_ref[m])
            change_1 = mul(left_1, mirror_1_ref[m])
            for i in range(b, b + size):
                part = slice((i - b) * width, (i - b + 1) * width)
                block = blocks_ref[i, m].astype(jnp.float32) - change_0[part]
                block = block.astype(jnp.bfloat16).astype(jnp.float32) - change_1[part]
                keep = (ids[i] >= PANELS) & (m * ids_ref[3] + ids_ref[1] >= PANELS)
                schur_here[i, m] = jnp.where(keep, block, 0.0).astype(jnp.bfloat16)
        for i in range(b, b + size):
            send(schur_here.at[i], schur_ref.at[i], schur_done.at[i])
    for copy in copies:
        copy.wait()


FACTOR_COST = pl.CostEstimate(flops=10**6, bytes_accessed=10**4, transcendentals=0)


def call_factor(kernel, name, shapes, *operands, scratch=()):
    in_specs = [
        pl.BlockSpec(memory_space=pltpu.SMEM if x.dtype == jnp.int32 else pltpu.VMEM) for x in operands]
    return pl.pallas_call(
        kernel, in_specs=in_specs, out_shape=shapes, scratch_shapes=scratch, name=name, cost_estimate=FACTOR_COST,
        compiler_params=pltpu.CompilerParams(vmem_limit_bytes=VMEM_LIMIT),
    )(*operands)


def square(width, dtype=jnp.float32):
    return jax.ShapeDtypeStruct((width, width), dtype)


def update(ids, column_0, column_1, blocks, mirror_0, later, lower_0, lower_1, pieces_0, pieces_1, panel_10):
    row_blocks, col_blocks, width = blocks.shape[:3]
    panels = jax.ShapeDtypeStruct((row_blocks, PANELS, width, width), jnp.float32)
    schur = jax.ShapeDtypeStruct(blocks.shape, jnp.bfloat16)
    return pl.pallas_call(
        update_kernel,
        in_specs=[pl.BlockSpec(memory_space=pltpu.SMEM)] + [pl.BlockSpec(memory_space=pltpu.VMEM)] * 10,
        out_specs=[pl.BlockSpec(memory_space=pl.ANY)] * 2,
        out_shape=[panels, schur],
        scratch_shapes=[
            pltpu.VMEM(panels.shape, panels.dtype),
            pltpu.VMEM(schur.shape, schur.dtype),
            pltpu.VMEM((col_blocks, width, width), jnp.bfloat16),
            pltpu.SemaphoreType.DMA((row_blocks, PANELS)),
            pltpu.SemaphoreType.DMA((row_blocks,)),
        ],
        compiler_params=pltpu.CompilerParams(vmem_limit_bytes=VMEM_LIMIT),
        cost_estimate=pl.CostEstimate(flops=2 * 10**9, bytes_accessed=6 * 10**6, transcendentals=0),
        name="solve_and_update",
    )(ids, column_0, column_1, blocks, mirror_0, later, lower_0, lower_1, pieces_0, pieces_1, panel_10)


def pack_kernel(kernel_ref, quarters_ref, semaphores):
    half = quarters_ref.shape[1]
    copies = []
    for q, (row, col) in enumerate(((0, 0), (1, 0), (1, 1))):
        source = kernel_ref.at[0, 0, 0, 0, pl.ds(row * half, half), pl.ds(col * half, half)]
        copies.append(pltpu.make_async_copy(source, quarters_ref.at[pl.ds(q * half, half)], semaphores.at[q]))
    for copy in copies:
        copy.start()
    for copy in copies:
        copy.wait()


def pack(kernel):
    half = kernel.shape[-1] // 2
    return pl.pallas_call(
        pack_kernel,
        in_specs=[pl.BlockSpec(memory_space=pltpu.HBM)],
        out_shape=jax.ShapeDtypeStruct((3 * half, half), kernel.dtype),
        scratch_shapes=[pltpu.SemaphoreType.DMA((3,))],
        compiler_params=pltpu.CompilerParams(vmem_limit_bytes=2 * 1024 * 1024),
        name="pack",
    )(kernel)


def swap(block, axis, distance):
    count = lax.axis_size(axis)
    return lax.ppermute(block, axis, [(d, d ^ distance) for d in range(count)])


HOLDERS = ((0, 0), (0, 1), (1, 0), (1, 1))


def diagonal_along(quarters, my_col):
    col_count = lax.axis_size("col")
    along = quarters
    for chip in range(1, col_count // 2):
        pairs = [(r * col_count + core, r * col_count + chip * 2 + core) for r, core in HOLDERS]
        got = lax.ppermute(quarters, ("row", "col"), pairs)
        along = jnp.where(my_col // 2 == chip, got, along)
    return along


def diagonal_down(along, my_row):
    first, second = along, along
    for step in range(1, lax.axis_size("row")):
        got = swap(along, "row", step)
        first = jnp.where(my_row == step, got, first)
        second = jnp.where(my_row == step ^ 1, got, second)
    return jnp.stack([first, second])


def both_cores(pair, my_col):
    other = swap(pair, "col", 1)
    even = my_col % 2 == 0
    left = jnp.where(even, pair, other)
    right = jnp.where(even, other, pair)
    return left[0], right[0], left[1], right[1]


def first_reach(block):
    return block, swap(block, "row", 2)


def other_reaches(block, got, my_row):
    reach = 2
    while True:
        block = jnp.where((my_row >= reach) & (my_row < 2 * reach), got, block)
        reach *= 2
        if reach >= lax.axis_size("row"):
            return block
        got = swap(block, "row", reach)


def first_stride(block):
    chips = lax.axis_size("col") // 2
    pairs = [(core, core + chips) for core in range(2)]
    return block, lax.ppermute(block, "col", pairs)


def other_strides(block, got, my_col):
    chips = lax.axis_size("col") // 2
    stride = chips // 2
    while True:
        block = jnp.where((my_col // 2) % (2 * stride) == stride, got, block)
        stride //= 2
        if stride == 0:
            return block
        if stride == 1:
            got = swap(block, "col", 2)
        else:
            sources = [chip * 2 + core for chip in range(0, chips, 2 * stride) for core in range(2)]
            got = lax.ppermute(block, "col", [(s, s + 2 * stride) for s in sources])


def per_device(kernel):
    my_row = lax.axis_index("row")
    my_col = lax.axis_index("col")
    even = my_col % 2 == 0
    blocks = kernel[0, :, 0]
    col_blocks, width = blocks.shape[1:3]
    half = width // 2
    ids = jnp.stack([my_row, my_col, lax.axis_size("row"), lax.axis_size("col")]).astype(jnp.int32)
    quarters = pack(kernel)
    rows, above, _ = lax.optimization_barrier((blocks[:, 0], blocks[0], quarters))
    rows, rows_got = first_stride(rows)
    above, above_got = first_reach(above)
    along = diagonal_along(quarters, my_col)
    pair = diagonal_down(along, my_row)
    pair, rows, rows_got = lax.optimization_barrier((pair, rows, rows_got))
    block_00, block_01, block_10, block_11 = both_cores(pair, my_col)
    rows = other_strides(rows, rows_got, my_col)
    upper_0, tile_inverse_0 = call_factor(start_kernel, "factor_start", [square(half)] * 2, block_00[:half])
    above, above_got, tile_inverse_0 = lax.optimization_barrier((above, above_got, tile_inverse_0))
    above = other_reaches(above, above_got, my_row)
    above_other = swap(above, "row", 1)
    pieces = jax.ShapeDtypeStruct((3, width, width), jnp.bfloat16)
    lower_0, pieces_0 = call_factor(
        first_kernel, "factor_first", [square(width), pieces], block_00[half:], upper_0, tile_inverse_0)
    panel_10, rest_11, upper_1, tile_inverse_1 = call_factor(
        second_start_kernel, "factor_second_start",
        [square(width, jnp.bfloat16), jax.ShapeDtypeStruct((width, half), jnp.bfloat16), square(half), square(half)],
        block_10[:half], block_10[half:], block_01[half:], block_11[:half], block_11[half:], pieces_0)
    rows, above, above_other, tile_inverse_1 = lax.optimization_barrier((rows, above, above_other, tile_inverse_1))
    other = swap(rows, "col", 1)
    mirror = jax.ShapeDtypeStruct((col_blocks, width, width), jnp.bfloat16)
    lower_1, pieces_1, mirror_0, later = call_factor(
        second_kernel, "factor_second", [square(width), pieces, mirror, mirror],
        ids, rest_11, upper_1, tile_inverse_1, pieces_0, panel_10, above, above_other,
        scratch=[pltpu.VMEM(mirror.shape, mirror.dtype)] * 2)
    other, lower_1 = lax.optimization_barrier((other, lower_1))
    column_0 = jnp.where(even, rows, other)
    column_1 = jnp.where(even, other, rows)
    panels, schur = update(
        ids, column_0, column_1, blocks, mirror_0, later, lower_0, lower_1, pieces_0, pieces_1, panel_10)
    return (panels[None], schur[None, :, None])


def solution(mesh):
    in_specs = (P("row", None, "col", None, None, None),)
    out_specs = (P("row", None, None, None, None), P("row", None, "col", None, None, None))
    return jax.shard_map(
        per_device, mesh=mesh, in_specs=in_specs, out_specs=out_specs, check_vma=False
    )
```

```python
import jax
import jax.numpy as jnp
from jax import lax
from jax.experimental import pallas as pl
from jax.experimental.pallas import tpu as pltpu
from jax.sharding import PartitionSpec as P

PANELS = 2
HIGHEST = lax.Precision.HIGHEST
VMEM_LIMIT = 20 * 1024 * 1024

def spread(row):
    return jnp.broadcast_to(row, (8, row.shape[1]))


def lane(tile, k):
    return jnp.broadcast_to(tile[:, k:k + 1], (8, 128))


def factor_tile(matrix, tasks=()):
    groups = 16
    rows_of = lax.broadcasted_iota(jnp.int32, (8, 128), 0)
    cols_of = lax.broadcasted_iota(jnp.int32, (8, 128), 1)
    left = [matrix[8 * g:8 * g + 8, :] for g in range(groups)]
    right = [(cols_of == rows_of + 8 * g).astype(jnp.float32) for g in range(groups)]
    upper, inverse = [], []
    for s in range(groups):
        y = [spread(left[s][k:k + 1, :]) for k in range(8)]
        v = [spread(right[s][k:k + 1, :]) for k in range(8)]
        d = [[lane(y[i], 8 * s + k) if k >= i else None for k in range(8)] for i in range(8)]
        last = s + 1 == groups
        near = None if last else [lane(left[s + 1], 8 * s + k) for k in range(8)]
        e = None if last else list(near)
        ratio = [[None] * 8 for _ in range(8)]
        inv = []
        for k in range(8):
            inv.append(pl.reciprocal(d[k][k], approx=True))
            for i in range(k + 1, 8):
                ratio[i][k] = d[k][i] * inv[k]
                for j in range(i, 8):
                    d[i][j] = d[i][j] - ratio[i][k] * d[k][j]
                y[i] = y[i] - ratio[i][k] * y[k]
                v[i] = v[i] - ratio[i][k] * v[k]
            if not last:
                left[s + 1] = left[s + 1] - e[k] * inv[k] * y[k]
                for j in range(k + 1, 8):
                    e[j] = e[j] - e[k] * ratio[j][k]
        up = jnp.zeros((8, 128), jnp.float32)
        low = jnp.zeros((8, 128), jnp.float32)
        for k in range(8):
            root = lax.rsqrt(d[k][k])
            up = jnp.where(rows_of == k, y[k] * root, up)
            low = jnp.where(rows_of == k, v[k] * root, low)
        upper.append(jnp.where(cols_of >= rows_of + 8 * s, up, 0.0))
        inverse.append(low)
        if s < len(tasks):
            tasks[s]()
        if last:
            break
        x, w = [None] * 8, [None] * 8
        for k in reversed(range(8)):
            x[k] = y[k] * inv[k]
            w[k] = v[k] * inv[k]
            for j in reversed(range(k + 1, 8)):
                x[k] = x[k] - ratio[j][k] * x[j]
                w[k] = w[k] - ratio[j][k] * w[j]
        for g in range(s + 1, groups):
            f = near if g == s + 1 else [lane(left[g], 8 * s + k) for k in range(8)]
            for k in reversed(range(8)):
                if g > s + 1:
                    left[g] = left[g] - f[k] * x[k]
                right[g] = right[g] - f[k] * w[k]
    return jnp.concatenate(upper, axis=0), jnp.concatenate(inverse, axis=0)


def dot(a, b, dims=((1,), (0,))):
    return lax.dot_general(a, b, (dims, ((), ())), precision=HIGHEST, preferred_element_type=jnp.float32)

ROWS = ((1,), (1,))

def mul(a, b, dims=((1,), (0,))):
    return lax.dot_general(a, b, (dims, ((), ())), preferred_element_type=jnp.float32)


def split(x):
    pieces = []
    for _ in range(3):
        pieces.append(x.astype(jnp.bfloat16))
        x = x - pieces[-1].astype(jnp.float32)
    return pieces


def product(pieces, block):
    return sum(mul(pieces[p], block) for p in (2, 1, 0))


def solve(rows, pieces):
    return sum(mul(rows, pieces[p], ROWS) for p in (2, 1, 0))


def factor_rest(upper_1, inv_1, side, rest, lower_ref, pieces_ref, tasks=()):
    half = side.shape[0]
    pieces = split(inv_1)
    lower_21 = solve(side, pieces)
    rest = rest.astype(jnp.float32) - dot(lower_21, lower_21, ROWS)
    beside = dot(lower_21, inv_1)

    def store_left():
        lower_ref[half:, :half] = lower_21
        lower_ref[:half, half:] = jnp.zeros((half, half), jnp.float32)
        lower_ref[:half, :half] = upper_1.T

    def store_pieces():
        for p in range(3):
            pieces_ref[p, :half, :half] = pieces[p]
            pieces_ref[p, :half, half:] = jnp.zeros((half, half), jnp.bfloat16)

    upper_2, inv_2 = factor_tile(rest, [store_left, store_pieces] + list(tasks))
    inv_21 = -dot(inv_2, beside)
    lower_ref[half:, half:] = upper_2.T
    for p, (left, right) in enumerate(zip(split(inv_21), split(inv_2))):
        pieces_ref[p, half:, :half] = left
        pieces_ref[p, half:, half:] = right


def start_kernel(quarter_ref, upper_ref, inverse_ref):
    upper, inverse = factor_tile(quarter_ref[...].astype(jnp.float32))
    upper_ref[...] = upper
    inverse_ref[...] = inverse


def first_kernel(rest_ref, upper_ref, tile_inverse_ref, lower_ref, pieces_ref):
    half = rest_ref.shape[1]
    factor_rest(upper_ref[...], tile_inverse_ref[...], rest_ref[:half], rest_ref[half:], lower_ref, pieces_ref)


def second_start_kernel(
    top_10_ref, rest_10_ref, rest_01_ref, top_11_ref, rest_11_ref, pieces_0_ref,
    panel_ref, later_ref, upper_ref, inverse_ref,
):
    half = top_11_ref.shape[1]
    corner = rest_01_ref[:half].astype(jnp.float32).T.astype(jnp.bfloat16)
    left = jnp.concatenate([top_10_ref[...], rest_10_ref[:half]], axis=0)
    right = jnp.concatenate([corner, rest_10_ref[half:]], axis=0)
    panel = solve(jnp.concatenate([left, right], axis=1), pieces_0_ref).astype(jnp.bfloat16)
    above, below = panel[:half], panel[half:]
    top = (top_11_ref[...].astype(jnp.float32) - mul(above, above, ROWS)).astype(jnp.bfloat16)

    def side():
        panel_ref[...] = panel
        later_ref[:half] = (rest_11_ref[:half].astype(jnp.float32) - mul(below, above, ROWS)).astype(jnp.bfloat16)

    def rest():
        later_ref[half:] = (rest_11_ref[half:].astype(jnp.float32) - mul(below, below, ROWS)).astype(jnp.bfloat16)

    upper, inverse = factor_tile(top.astype(jnp.float32), (side, rest))
    upper_ref[...] = upper
    inverse_ref[...] = inverse


def second_kernel(
    rest_ref, upper_ref, tile_inverse_ref, pieces_0_ref, panel_ref, above_ref, other_ref,
    lower_ref, pieces_1_ref, mirror_ref, later_ref, above_0_ref, above_1_ref,
):
    half = rest_ref.shape[1]
    even = lax.rem(lax.axis_index("row"), 2) == 0
    tasks = []

    @pl.when(even)
    def _():
        above_0_ref[...] = above_ref[...]
        above_1_ref[...] = other_ref[...]

    @pl.when(jnp.logical_not(even))
    def _():
        above_0_ref[...] = other_ref[...]
        above_1_ref[...] = above_ref[...]

    parts = (pl.ds(0, half), pl.ds(half, half))
    for m in range(above_ref.shape[0]):
        for part in parts:
            def mirror(m=m, part=part):
                terms = [mul(pieces_0_ref[p, part], above_0_ref[m]) for p in (2, 1, 0)]
                mirror_ref[m, part] = sum(terms).astype(jnp.bfloat16)
            tasks.append(mirror)
    for m in range(above_ref.shape[0]):
        for part in parts:
            def later(m=m, part=part):
                change = mul(panel_ref[part], mirror_ref[m])
                later_ref[m, part] = (above_1_ref[m, part].astype(jnp.float32) - change).astype(jnp.bfloat16)
            tasks.append(later)
    factor_rest(
        upper_ref[...], tile_inverse_ref[...], rest_ref[:half], rest_ref[half:], lower_ref, pieces_1_ref, tasks)


def update_kernel(
    column_0_ref, column_1_ref, blocks_ref, mirror_0_ref, later_ref,
    lower_0_ref, lower_1_ref, pieces_0_ref, pieces_1_ref, panel_10_ref,
    panels_ref, schur_ref, panels_here, schur_here, mirror_1_ref, panels_done, schur_done,
):
    row_blocks, col_blocks, width = blocks_ref.shape[:3]
    size = 2 if row_blocks % 2 == 0 else 1
    batches = range(0, row_blocks, size)
    row_count, col_count = lax.axis_size("row"), lax.axis_size("col")
    my_row, my_col = lax.axis_index("row"), lax.axis_index("col")
    ids = [i * row_count + my_row for i in range(row_blocks)]
    copies = []

    def send(source, target, semaphore):
        copies.append(pltpu.make_async_copy(source, target, semaphore))
        copies[-1].start()

    def below(solved, panel, lower_ref, start):
        parts = []
        for i in range(start, start + size):
            part = jnp.where(ids[i] > panel, solved[(i - start) * width:(i - start + 1) * width], 0.0)
            panels_here[i, panel] = jnp.where(ids[i] == panel, lower_ref[...], part)
            send(panels_here.at[i, panel], panels_ref.at[i, panel], panels_done.at[i, panel])
            parts.append(part)
        return jnp.concatenate(parts, axis=0).astype(jnp.bfloat16)

    def batch(column_ref, start):
        return column_ref[start:start + size].reshape(size * width, width)

    rounded_0 = [below(solve(batch(column_0_ref, b), pieces_0_ref), 0, lower_0_ref, b) for b in batches]
    columns = []
    for b, rounded in zip(batches, rounded_0):
        change = mul(rounded, panel_10_ref[...], ROWS)
        columns.append((batch(column_1_ref, b).astype(jnp.float32) - change).astype(jnp.bfloat16))
    for m in range(col_blocks):
        mirror_1_ref[m] = product(pieces_1_ref, later_ref[m]).astype(jnp.bfloat16)
    rounded_1 = [below(solve(column, pieces_1_ref), 1, lower_1_ref, b) for b, column in zip(batches, columns)]
    for b, left_0, left_1 in zip(batches, rounded_0, rounded_1):
        for m in range(col_blocks):
            change_0 = mul(left_0, mirror_0_ref[m])
            change_1 = mul(left_1, mirror_1_ref[m])
            for i in range(b, b + size):
                part = slice((i - b) * width, (i - b + 1) * width)
                block = blocks_ref[i, m].astype(jnp.float32) - change_0[part]
                block = block.astype(jnp.bfloat16).astype(jnp.float32) - change_1[part]
                keep = (ids[i] >= PANELS) & (m * col_count + my_col >= PANELS)
                schur_here[i, m] = jnp.where(keep, block, 0.0).astype(jnp.bfloat16)
        for i in range(b, b + size):
            send(schur_here.at[i], schur_ref.at[i], schur_done.at[i])
    for copy in copies:
        copy.wait()


FACTOR_COST = pl.CostEstimate(flops=10**6, bytes_accessed=10**4, transcendentals=0)


def call_factor(kernel, name, shapes, *operands, scratch=()):
    in_specs = [pl.BlockSpec(memory_space=pltpu.VMEM)] * len(operands)
    return pl.pallas_call(
        kernel, in_specs=in_specs, out_shape=shapes, scratch_shapes=scratch, name=name, cost_estimate=FACTOR_COST,
        compiler_params=pltpu.CompilerParams(vmem_limit_bytes=VMEM_LIMIT),
    )(*operands)


def square(width, dtype=jnp.float32):
    return jax.ShapeDtypeStruct((width, width), dtype)


def update(column_0, column_1, blocks, mirror_0, later, lower_0, lower_1, pieces_0, pieces_1, panel_10):
    row_blocks, col_blocks, width = blocks.shape[:3]
    panels = jax.ShapeDtypeStruct((row_blocks, PANELS, width, width), jnp.float32)
    schur = jax.ShapeDtypeStruct(blocks.shape, jnp.bfloat16)
    return pl.pallas_call(
        update_kernel,
        in_specs=[pl.BlockSpec(memory_space=pltpu.VMEM)] * 10,
        out_specs=[pl.BlockSpec(memory_space=pl.ANY)] * 2,
        out_shape=[panels, schur],
        scratch_shapes=[
            pltpu.VMEM(panels.shape, panels.dtype),
            pltpu.VMEM(schur.shape, schur.dtype),
            pltpu.VMEM((col_blocks, width, width), jnp.bfloat16),
            pltpu.SemaphoreType.DMA((row_blocks, PANELS)),
            pltpu.SemaphoreType.DMA((row_blocks,)),
        ],
        compiler_params=pltpu.CompilerParams(vmem_limit_bytes=VMEM_LIMIT),
        cost_estimate=pl.CostEstimate(flops=2 * 10**9, bytes_accessed=6 * 10**6, transcendentals=0),
        name="solve_and_update",
    )(column_0, column_1, blocks, mirror_0, later, lower_0, lower_1, pieces_0, pieces_1, panel_10)


def pack_kernel(kernel_ref, quarters_ref, semaphores):
    half = quarters_ref.shape[1]
    copies = []
    for q, (row, col) in enumerate(((0, 0), (1, 0), (1, 1))):
        source = kernel_ref.at[0, 0, 0, 0, pl.ds(row * half, half), pl.ds(col * half, half)]
        copies.append(pltpu.make_async_copy(source, quarters_ref.at[pl.ds(q * half, half)], semaphores.at[q]))
    for copy in copies:
        copy.start()
    for copy in copies:
        copy.wait()


def pack(kernel):
    half = kernel.shape[-1] // 2
    return pl.pallas_call(
        pack_kernel,
        in_specs=[pl.BlockSpec(memory_space=pltpu.HBM)],
        out_shape=jax.ShapeDtypeStruct((3 * half, half), kernel.dtype),
        scratch_shapes=[pltpu.SemaphoreType.DMA((3,))],
        compiler_params=pltpu.CompilerParams(vmem_limit_bytes=2 * 1024 * 1024),
        name="pack",
    )(kernel)


def swap(block, axis, distance):
    count = lax.axis_size(axis)
    return lax.ppermute(block, axis, [(d, d ^ distance) for d in range(count)])


HOLDERS = ((0, 0), (0, 1), (1, 0), (1, 1))


def diagonal_along(quarters, my_col):
    col_count = lax.axis_size("col")
    along = quarters
    for chip in range(1, col_count // 2):
        pairs = [(r * col_count + core, r * col_count + chip * 2 + core) for r, core in HOLDERS]
        got = lax.ppermute(quarters, ("row", "col"), pairs)
        along = jnp.where(my_col // 2 == chip, got, along)
    return along


def diagonal_down(along, my_row):
    first, second = along, along
    for step in range(1, lax.axis_size("row")):
        got = swap(along, "row", step)
        first = jnp.where(my_row == step, got, first)
        second = jnp.where(my_row == step ^ 1, got, second)
    return jnp.stack([first, second])


def both_cores(pair, my_col):
    other = swap(pair, "col", 1)
    even = my_col % 2 == 0
    left = jnp.where(even, pair, other)
    right = jnp.where(even, other, pair)
    return left[0], right[0], left[1], right[1]


def first_reach(block):
    return block, swap(block, "row", 2)


def other_reaches(block, got, my_row):
    reach = 2
    while True:
        block = jnp.where((my_row >= reach) & (my_row < 2 * reach), got, block)
        reach *= 2
        if reach >= lax.axis_size("row"):
            return block
        got = swap(block, "row", reach)


def first_stride(block):
    chips = lax.axis_size("col") // 2
    pairs = [(core, core + chips) for core in range(2)]
    return block, lax.ppermute(block, "col", pairs)


def other_strides(block, got, my_col):
    chips = lax.axis_size("col") // 2
    stride = chips // 2
    while True:
        block = jnp.where((my_col // 2) % (2 * stride) == stride, got, block)
        stride //= 2
        if stride == 0:
            return block
        if stride == 1:
            got = swap(block, "col", 2)
        else:
            sources = [chip * 2 + core for chip in range(0, chips, 2 * stride) for core in range(2)]
            got = lax.ppermute(block, "col", [(s, s + 2 * stride) for s in sources])


def per_device(kernel):
    my_row = lax.axis_index("row")
    my_col = lax.axis_index("col")
    even = my_col % 2 == 0
    blocks = kernel[0, :, 0]
    col_blocks, width = blocks.shape[1:3]
    half = width // 2
    quarters = pack(kernel)
    rows, above, _ = lax.optimization_barrier((blocks[:, 0], blocks[0], quarters))
    rows, rows_got = first_stride(rows)
    above, above_got = first_reach(above)
    along = diagonal_along(quarters, my_col)
    pair = diagonal_down(along, my_row)
    pair, rows, rows_got = lax.optimization_barrier((pair, rows, rows_got))
    block_00, block_01, block_10, block_11 = both_cores(pair, my_col)
    rows = other_strides(rows, rows_got, my_col)
    upper_0, tile_inverse_0 = call_factor(start_kernel, "factor_start", [square(half)] * 2, block_00[:half])
    above, above_got, tile_inverse_0 = lax.optimization_barrier((above, above_got, tile_inverse_0))
    above = other_reaches(above, above_got, my_row)
    above_other = swap(above, "row", 1)
    pieces = jax.ShapeDtypeStruct((3, width, width), jnp.bfloat16)
    lower_0, pieces_0 = call_factor(
        first_kernel, "factor_first", [square(width), pieces], block_00[half:], upper_0, tile_inverse_0)
    panel_10, rest_11, upper_1, tile_inverse_1 = call_factor(
        second_start_kernel, "factor_second_start",
        [square(width, jnp.bfloat16), jax.ShapeDtypeStruct((width, half), jnp.bfloat16), square(half), square(half)],
        block_10[:half], block_10[half:], block_01[half:], block_11[:half], block_11[half:], pieces_0)
    rows, above, above_other, tile_inverse_1 = lax.optimization_barrier((rows, above, above_other, tile_inverse_1))
    other = swap(rows, "col", 1)
    mirror = jax.ShapeDtypeStruct((col_blocks, width, width), jnp.bfloat16)
    lower_1, pieces_1, mirror_0, later = call_factor(
        second_kernel, "factor_second", [square(width), pieces, mirror, mirror],
        rest_11, upper_1, tile_inverse_1, pieces_0, panel_10, above, above_other,
        scratch=[pltpu.VMEM(mirror.shape, mirror.dtype)] * 2)
    other, lower_1 = lax.optimization_barrier((other, lower_1))
    column_0 = jnp.where(even, rows, other)
    column_1 = jnp.where(even, other, rows)
    panels, schur = update(
        column_0, column_1, blocks, mirror_0, later, lower_0, lower_1, pieces_0, pieces_1, panel_10)
    return (panels[None], schur[None, :, None])


def solution(mesh):
    in_specs = (P("row", None, "col", None, None, None),)
    out_specs = (P("row", None, None, None, None), P("row", None, "col", None, None, None))
    return jax.shard_map(
        per_device, mesh=mesh, in_specs=in_specs, out_specs=out_specs, check_vma=False
    )
```
